32 devices in a mesh: rep: 4 (over y, x), tr: 4 (over z), tc: 2 (over core).
Axes of the slice: x: 2, y: 2, z: 4, core: 2. Of those that a mesh axis runs over, the one named last changes fastest.
Arguments:
- tokens: bfloat16 [128, 16, 8, 1600], P(('rep', 'tr'), None, None, 'tc'), may hold values from -6 to 6
- prefix_kv: bfloat16 [128, 256, 512], P(('rep', 'tr'), None, 'tc')
- ssm_state: float32 [128, 16, 3200], P(('rep', 'tr'), None, 'tc'), may hold values from -6 to 6
- conv_state: float32 [128, 3, 3200], P(('rep', 'tr'), None, 'tc'), may hold values from -6 to 6
- prefix_len: int32 [128], replicated, may hold values from 1 to 256
- group_size: int32 [128], replicated, may hold values from 8 to 16
- serve_replica: int32 [128], replicated, may hold values from 0 to 3, as said below
- in_gain: float32 [1600], P('tc'), may hold values from 0.5 to 1.5
- w_query: bfloat16 [1600, 1024], P(('rep', 'tr'), 'tc'), may hold values from -0.15625 to 0.15625
- w_keyval: bfloat16 [1600, 512], P(('rep', 'tr'), 'tc'), may hold values from -0.15625 to 0.15625
- w_inner: bfloat16 [1600, 2, 3200], P(('rep', 'tr'), None, 'tc'), may hold values from -0.15625 to 0.15625
- conv_weight: float32 [4, 3200], P(None, 'tc'), may hold values from -3 to 3
- conv_bias: float32 [3200], P('tc'), may hold values from -3 to 3
- w_xproj: bfloat16 [3200, 132], P('tc'), may hold values from -0.109375 to 0.109375
- dt_weight: bfloat16 [100, 3200], P(None, 'tc'), may hold values from -0.625 to 0.625
- dt_bias: float32 [3200], P('tc'), may hold values from -4.5 to -1
- decay_log: float32 [16, 3200], P(None, 'tc'), may hold values from -1 to 2.5
- skip_gain: float32 [3200], P('tc'), may hold values from 0.5 to 1.5
- w_attn_out: bfloat16 [1024, 1600], P('tc', ('rep', 'tr'))
- w_ssm_out: bfloat16 [3200, 1600], P('tc', ('rep', 'tr'))
- attn_gain: float32 [1600], replicated, may hold values from 0.5 to 1.5
- ssm_gain: float32 [1600], replicated, may hold values from 0.5 to 1.5
Outputs:
- mixed: bfloat16 [128, 16, 8, 1600], P(('rep', 'tr'), None, None, 'tc')
The draws below stay inside these ranges and needn't reach their ends.
Inputs may be any that keep to these rules, and one draw needn't show every extreme that they name: `serve_replica`: within each aligned block of 8 groups every replica is named equally often.
All inputs are finite; a program needn't handle non-finite values.
Results may differ from the reference program's by a relative error of at most 0.013.
Values may be sent and summed in bfloat16 or wider, within the bound.
No kernel may reach another device: no remote copies, remote signals or barrier semaphores. Data moves between devices by JAX's collectives and lax.ppermute only.
A program may use at most 192 MiB of HBM per device.

```python
import jax
import jax.numpy as jnp
from jax import lax

D = 1600
HD = 64
QH = 16
KVH = 4
DI = 3200
N = 16
R = 100
KC = 4
GMAX = 16
NEW = 8
G_DEV = 8
PMAX = 256
GROUPS = 128
N_REP = 4
N_TR = 4
N_TC = 2


def draw_serve_replica(key, part):
    block_total = GROUPS // G_DEV
    keys_all = jax.random.split(key, block_total)
    cycle_ids = jnp.arange(G_DEV, dtype=jnp.int32) % N_REP
    blocks = jax.vmap(lambda subkey: jax.random.permutation(subkey, cycle_ids))(keys_all)
    return blocks.reshape(GROUPS).astype(jnp.int32)


def draw_prefix_len(key, part):
    key_one, key_two, key_three, key_top, key_low = jax.random.split(key, 5)
    lengths = jax.random.randint(key_one, (GROUPS,), 1, PMAX + 1)
    lengths = jnp.minimum(lengths, jax.random.randint(key_two, (GROUPS,), 1, PMAX + 1))
    lengths = jnp.minimum(lengths, jax.random.randint(key_three, (GROUPS,), 1, PMAX + 1))
    top_at = jax.random.randint(key_top, (), 0, GROUPS)
    low_at = (top_at + jax.random.randint(key_low, (), 1, GROUPS)) % GROUPS
    lengths = lengths.at[top_at].set(PMAX).at[low_at].set(1)
    return lengths.astype(jnp.int32)


def draw_group_size(key, part):
    key_main, key_top, key_low = jax.random.split(key, 3)
    counts = jax.random.randint(key_main, (GROUPS,), GMAX // 2, GMAX + 1)
    top_at = jax.random.randint(key_top, (), 0, GROUPS)
    low_at = (top_at + jax.random.randint(key_low, (), 1, GROUPS)) % GROUPS
    counts = counts.at[top_at].set(GMAX).at[low_at].set(GMAX // 2)
    return counts.astype(jnp.int32)


def draw_prefix_kv(key, part):
    key_main = jax.random.fold_in(key, 0)
    shape_all = (GROUPS, PMAX, KVH * 2 * HD)
    values = jax.random.normal(key_main, shape_all, jnp.float32)
    return values.astype(jnp.bfloat16)


def rising_columns(key, rows, columns):
    position = jnp.arange(columns, dtype=jnp.float32) / (columns - 1) - 0.5
    values = jax.random.normal(key, (rows, columns), jnp.float32)
    ramp = jnp.exp(jnp.log(8.0) * position)
    return (values * ramp[None, :] * rows ** (-0.5)).astype(jnp.bfloat16)


def draw_w_attn_out(key, part):
    return rising_columns(jax.random.fold_in(key, 11), QH * HD, D)


def draw_w_ssm_out(key, part):
    return rising_columns(jax.random.fold_in(key, 12), DI, D)


def block_scale(stream_key, shape, shards, smallest, top_value):
    level = 1.0
    for dim, blocks in shards:
        steps = jax.random.uniform(jax.random.fold_in(jax.random.fold_in(stream_key, 6), dim), (blocks,), jnp.float32, smallest / len(shards), top_value / len(shards))
        level = level * jnp.repeat(jnp.exp(steps), shape[dim] // blocks).reshape((-1,) + (1,) * (len(shape) - 1 - dim))
    return level


def bell_draw(stream_key, extent, spread, bound, cuts=(), kind=jnp.bfloat16):
    values = spread * jax.random.normal(stream_key, extent, jnp.float32)
    if cuts:
        values = values * block_scale(stream_key, extent, cuts, -0.22, 0.18)
    return jnp.clip(values, -bound, bound).astype(kind)


def setup_inputs(seed: int = 0) -> dict:
    keys = jax.random.split(jax.random.key(seed), 23)
    tokens = bell_draw(keys[0], (GROUPS, GMAX, NEW, D), 1.0, 6.0, ((0, 16), (3, 2)))
    prefix_kv = draw_prefix_kv(jax.random.fold_in(keys[22], 71), 0)
    ssm_state = bell_draw(keys[2], (GROUPS, N, DI), 1.0, 6.0, ((0, 16), (2, 2)), jnp.float32)
    conv_state = bell_draw(keys[3], (GROUPS, KC - 1, DI), 1.0, 6.0, ((0, 16), (2, 2)), jnp.float32)
    prefix_len = draw_prefix_len(jax.random.fold_in(keys[22], 71), 0)
    group_size = draw_group_size(jax.random.fold_in(keys[22], 71), 0)
    serve_replica = draw_serve_replica(jax.random.fold_in(keys[22], 71), 0)
    in_gain = jnp.clip(1.0 + 0.1 * jax.random.normal(keys[7], (D,), jnp.float32), 0.5, 1.5)
    w_query = bell_draw(keys[8], (D, QH * HD), D ** -0.5, 0.15625, ((0, 16), (1, 2)))
    w_keyval = bell_draw(keys[9], (D, KVH * 2 * HD), D ** -0.5, 0.15625, ((0, 16), (1, 2)))
    w_inner = bell_draw(keys[10], (D, 2, DI), D ** -0.5, 0.15625, ((0, 16), (2, 2)))
    conv_weight = bell_draw(keys[11], (KC, DI), KC ** -0.5, 3.0, ((1, 2),), jnp.float32)
    conv_bias = bell_draw(keys[12], (DI,), 0.5, 3.0, ((0, 2),), jnp.float32)
    w_xproj = bell_draw(keys[13], (DI, R + 2 * N), DI ** -0.5, 0.109375, ((0, 2),))
    dt_weight = bell_draw(keys[14], (R, DI), R ** -0.5, 0.625, ((1, 2),))
    dt_bias = jnp.clip(-4.5 + 3.5 * jax.random.uniform(keys[15], (DI,), jnp.float32) ** block_scale(keys[15], (DI,), ((0, 2),), -0.2, 0.2), -4.5, -1.0)
    decay_log = jnp.clip(-1.0 + 3.5 * jax.random.uniform(keys[16], (N, DI), jnp.float32) ** block_scale(keys[16], (N, DI), ((1, 2),), -0.2, 0.2), -1.0, 2.5)
    skip_gain = jnp.clip(0.5 + 1.0 * jax.random.uniform(keys[17], (DI,), jnp.float32) ** block_scale(keys[17], (DI,), ((0, 2),), -0.2, 0.2), 0.5, 1.5)
    w_attn_out = draw_w_attn_out(jax.random.fold_in(keys[22], 71), 0)
    w_ssm_out = draw_w_ssm_out(jax.random.fold_in(keys[22], 71), 0)
    attn_gain = jnp.clip(1.0 + 0.1 * jax.random.normal(keys[20], (D,), jnp.float32), 0.5, 1.5)
    ssm_gain = jnp.clip(1.0 + 0.1 * jax.random.normal(keys[21], (D,), jnp.float32), 0.5, 1.5)
    return {"tokens": tokens, "prefix_kv": prefix_kv, "ssm_state": ssm_state, "conv_state": conv_state, "prefix_len": prefix_len, "group_size": group_size, "serve_replica": serve_replica, "in_gain": in_gain, "w_query": w_query, "w_keyval": w_keyval, "w_inner": w_inner, "conv_weight": conv_weight, "conv_bias": conv_bias, "w_xproj": w_xproj, "dt_weight": dt_weight, "dt_bias": dt_bias, "decay_log": decay_log, "skip_gain": skip_gain, "w_attn_out": w_attn_out, "w_ssm_out": w_ssm_out, "attn_gain": attn_gain, "ssm_gain": ssm_gain}


EPSILON = 1e-06

def shared_sum(activity, weight, shares):
    share_width = activity.shape[1] // shares
    running = jnp.zeros((activity.shape[0], weight.shape[1]), jnp.float32)
    for share_index in range(shares):
        lower = share_index * share_width
        partial_value = jnp.dot(activity[:, lower:lower + share_width], weight[lower:lower + share_width], preferred_element_type=jnp.float32)
        running = running + lax.optimization_barrier(partial_value.astype(jnp.bfloat16)).astype(jnp.float32)
    return running

def reference(tokens, prefix_kv, ssm_state, conv_state, prefix_len, group_size, serve_replica, in_gain, w_query, w_keyval, w_inner, conv_weight, conv_bias, w_xproj, dt_weight, dt_bias, decay_log, skip_gain, w_attn_out, w_ssm_out, attn_gain, ssm_gain):
    group_total = tokens.shape[0]
    row_count = GMAX * NEW
    score_scale = HD ** (-0.5)
    causal = jnp.arange(NEW)[None, :] <= jnp.arange(NEW)[:, None]
    inner_weight = w_inner.reshape(D, 2 * DI)
    decay_rate = -jnp.exp(decay_log)

    def layer_group(group_args):
        group_tokens, group_cache, group_state, group_conv, length, live_count = group_args
        x_rows = group_tokens.reshape(row_count, D).astype(jnp.float32)
        inv_rms = lax.rsqrt(lax.optimization_barrier(jnp.mean(x_rows * x_rows, axis=1, keepdims=True)) + EPSILON)
        normed = (x_rows * inv_rms * in_gain).astype(jnp.bfloat16)
        query = jnp.dot(normed, w_query, preferred_element_type=jnp.float32).astype(jnp.bfloat16)
        query_f = query.reshape(GMAX, NEW, KVH, QH // KVH, HD).astype(jnp.float32)
        keyval = jnp.dot(normed, w_keyval, preferred_element_type=jnp.float32).astype(jnp.bfloat16)
        keyval = keyval.reshape(GMAX, NEW, KVH, 2, HD).astype(jnp.float32)
        cache = group_cache.reshape(PMAX, KVH, 2, HD).astype(jnp.float32)
        prefix_scores = jnp.einsum('rtkjd,pkd->rtkjp', query_f, cache[:, :, 0]) * score_scale
        own_scores = jnp.einsum('rtkjd,rskd->rtkjs', query_f, keyval[:, :, :, 0]) * score_scale
        allowed = jnp.arange(PMAX) < length
        prefix_scores = jnp.where(allowed, prefix_scores, -jnp.inf)
        own_scores = jnp.where(causal[None, :, None, None, :], own_scores, -jnp.inf)
        row_max = jnp.maximum(lax.optimization_barrier(jnp.max(prefix_scores, axis=4)), lax.optimization_barrier(jnp.max(own_scores, axis=4)))[..., None]
        prefix_weights = jnp.exp(prefix_scores - row_max)
        own_weights = jnp.exp(own_scores - row_max)
        totals = lax.optimization_barrier(jnp.sum(prefix_weights, axis=4)) + lax.optimization_barrier(jnp.sum(own_weights, axis=4))
        weighted = jnp.einsum('rtkjp,pkd->rtkjd', prefix_weights.astype(jnp.bfloat16).astype(jnp.float32), cache[:, :, 1])
        weighted = weighted + jnp.einsum('rtkjs,rskd->rtkjd', own_weights.astype(jnp.bfloat16).astype(jnp.float32), keyval[:, :, :, 1])
        heads = (weighted / totals[..., None]).astype(jnp.bfloat16).reshape(row_count, QH * HD)
        inner = jnp.dot(normed, inner_weight, preferred_element_type=jnp.float32).reshape(GMAX, NEW, 2, DI)
        conv_in = inner[:, :, 0]
        gate = inner[:, :, 1].reshape(row_count, DI)
        history = jnp.broadcast_to(group_conv[None], (GMAX, KC - 1, DI))
        sequence = jnp.concatenate([history, conv_in], axis=1)
        conv_sum = jnp.broadcast_to(conv_bias, (GMAX, NEW, DI))
        for tap_index in range(KC):
            conv_sum = conv_sum + conv_weight[tap_index] * sequence[:, tap_index:tap_index + NEW]
        conv_out = jax.nn.silu(conv_sum).astype(jnp.bfloat16).reshape(row_count, DI)
        projected = jnp.dot(conv_out, w_xproj, preferred_element_type=jnp.float32)
        step_in = projected[:, :R].astype(jnp.bfloat16)
        input_mix = projected[:, R:R + N]
        output_mix = projected[:, R + N:]
        step_size = jax.nn.softplus(jnp.dot(step_in, dt_weight, preferred_element_type=jnp.float32) + dt_bias)

        def token_major(values):
            return values.reshape(GMAX, NEW, values.shape[1]).swapaxes(0, 1)
        start_state = jnp.broadcast_to(group_state[None], (GMAX, N, DI))

        def advance(carried, inputs):
            step_now, value_now, mix_in, mix_out = inputs
            carried = jnp.exp(step_now[:, None, :] * decay_rate[None]) * carried + (step_now * value_now)[:, None, :] * mix_in[:, :, None]
            result = lax.optimization_barrier(jnp.sum(carried * mix_out[:, :, None], axis=1)) + skip_gain * value_now
            return (carried, result)
        last_state, outputs = lax.scan(advance, start_state, (token_major(step_size), token_major(conv_out.astype(jnp.float32)), token_major(input_mix), token_major(output_mix)))
        ssm_out = outputs.swapaxes(0, 1).reshape(row_count, DI)
        gated = (ssm_out * jax.nn.silu(gate)).astype(jnp.bfloat16)
        attn_sum = shared_sum(heads, w_attn_out, N_TC)
        ssm_sum = shared_sum(gated, w_ssm_out, N_TC)
        attn_rms = lax.rsqrt(lax.optimization_barrier(jnp.mean(attn_sum * attn_sum, axis=1, keepdims=True)) + EPSILON)
        ssm_rms = lax.rsqrt(lax.optimization_barrier(jnp.mean(ssm_sum * ssm_sum, axis=1, keepdims=True)) + EPSILON)
        mixed = x_rows + 0.5 * (attn_gain * attn_sum * attn_rms + ssm_gain * ssm_sum * ssm_rms)
        live = jnp.arange(GMAX) < live_count
        live_rows = jnp.broadcast_to(live[:, None], (GMAX, NEW)).reshape(row_count, 1)
        return jnp.where(live_rows, mixed, 0.0).astype(jnp.bfloat16).reshape(GMAX, NEW, D)
    mixed = lax.map(layer_group, (tokens, prefix_kv, ssm_state, conv_state, prefix_len, group_size))
    group_ids = jnp.arange(group_total, dtype=jnp.int32)
    row_position = group_ids // G_DEV % N_TR
    order = jnp.argsort((serve_replica * N_TR + row_position) * group_total + group_ids, stable=True).astype(jnp.int32)
    return jnp.take(mixed, order, axis=0)
```

```python
import functools

import jax
import jax.numpy as jnp
import numpy as np
from jax import lax
from jax.experimental import pallas as pl
from jax.experimental.pallas import tpu as pltpu
from jax.sharding import PartitionSpec as P

D = 1600
HD = 64
QH = 16
KVH = 4

EPSILON = 1e-06
LOG2_E = 1.4426950408889634

X_PAIRS = ((0, 1), (1, 0), (2, 3), (3, 2))
Y_PAIRS = ((0, 2), (2, 0), (1, 3), (3, 1))
D_PAIRS = ((0, 3), (3, 0), (1, 2), (2, 1))
Z_OUTER = ((0, 1), (1, 0), (2, 3), (3, 2))
Z_INNER = ((1, 2), (2, 1))
Z_ENDS = ((1, 0), (2, 3))
Z_FAR = ((2, 0), (1, 3))
Z_SLOTS = ((0, 1, 2, 3), (1, 0, 2, 3), (2, 3, 1, 0), (3, 2, 1, 0))

VMEM_LIMIT = 56 * 1024 * 1024


def params():
    return pltpu.CompilerParams(vmem_limit_bytes=VMEM_LIMIT)


def cost(flops, size):
    return pl.CostEstimate(flops=int(flops), bytes_accessed=int(size), transcendentals=0)


def after(values, earlier):
    count = len(values)
    return lax.optimization_barrier(tuple(values) + tuple(earlier))[:count]


def swap_x(value):
    return lax.ppermute(value, "rep", X_PAIRS)


def swap_y(value):
    return lax.ppermute(value, "rep", Y_PAIRS)


def along_z(value, pairs):
    return lax.ppermute(value, "tr", pairs)


def other_core(value):
    return lax.ppermute(value, "tc", ((0, 1), (1, 0)))


def load_rows(pieces, target, sems, starts):
    copies = []
    for index, (piece, start) in enumerate(zip(pieces, starts)):
        copies.append(
            pltpu.make_async_copy(
                piece, target.at[pl.ds(start, piece.shape[0]), :], sems.at[index]
            )
        )
    for copy in copies:
        copy.start()
    return copies


def row_starts(pieces):
    starts = [0]
    for piece in pieces:
        starts.append(starts[-1] + piece.shape[0])
    return starts[:-1]


def spread_kernel(own, other, x_own, a_own, a_other, b_own, b_other, keep, out_a, out_b, out_x):
    mine = own[...]
    theirs = other[...]

    def both(first, second):
        return jnp.dot(mine, first[...], preferred_element_type=jnp.float32) + jnp.dot(
            theirs, second[...], preferred_element_type=jnp.float32
        )

    out_a[...] = both(a_own, a_other).astype(jnp.bfloat16)
    out_b[...] = both(b_own, b_other).astype(jnp.bfloat16)
    out_x[...] = jnp.dot(x_own[...], keep[...], preferred_element_type=jnp.float32).astype(
        jnp.bfloat16
    )


def attention_kernel(
    slots, kv_here, per_kv, count, lengths, rows, cache, *rest
):
    pieces, (out, weight, sems) = rest[:count], rest[count:]
    group = pl.program_id(0)

    @pl.when(group == 0)
    def _():
        for copy in load_rows(pieces, weight, sems, row_starts(pieces)):
            copy.wait()

    length = lengths[group]
    made = jnp.dot(rows[...], weight[...], preferred_element_type=jnp.float32).astype(jnp.bfloat16)
    total_rows = made.shape[0]
    query_width = kv_here * per_kv * HD
    positions = cache.shape[1]
    stacked = per_kv * total_rows
    row_id = lax.broadcasted_iota(jnp.int32, (stacked, total_rows), 0) % total_rows
    column_id = lax.broadcasted_iota(jnp.int32, (stacked, total_rows), 1)
    own_mask = (row_id % slots == column_id % slots) & (column_id // slots <= row_id // slots)
    prefix_mask = lax.broadcasted_iota(jnp.int32, (stacked, positions), 1) < length
    contract = (((1,), (1,)), ((), ()))
    results = []
    for head in range(kv_here):
        query = jnp.concatenate(
            [
                made[:, (head * per_kv + j) * HD : (head * per_kv + j + 1) * HD]
                for j in range(per_kv)
            ],
            axis=0,
        )
        base = query_width + head * 2 * HD
        key_new = made[:, base : base + HD]
        value_new = made[:, base + HD : base + 2 * HD]
        key_old = cache[0, :, head * 2 * HD : head * 2 * HD + HD]
        value_old = cache[0, :, head * 2 * HD + HD : (head + 1) * 2 * HD]
        scale = HD ** (-0.5)
        old = lax.dot_general(query, key_old, contract, preferred_element_type=jnp.float32) * scale
        new = lax.dot_general(query, key_new, contract, preferred_element_type=jnp.float32) * scale
        old = jnp.where(prefix_mask, old, -jnp.inf)
        new = jnp.where(own_mask, new, -jnp.inf)
        top = jnp.maximum(
            jnp.max(old, axis=1, keepdims=True), jnp.max(new, axis=1, keepdims=True)
        )
        old = jnp.exp(old - top)
        new = jnp.exp(new - top)
        total = jnp.sum(old, axis=1, keepdims=True) + jnp.sum(new, axis=1, keepdims=True)
        value = jnp.dot(
            old.astype(jnp.bfloat16), value_old, preferred_element_type=jnp.float32
        ) + jnp.dot(new.astype(jnp.bfloat16), value_new, preferred_element_type=jnp.float32)
        value = (value / total).astype(jnp.bfloat16)
        for j in range(per_kv):
            results.append(value[j * total_rows : (j + 1) * total_rows])
    out[...] = jnp.concatenate(results, axis=1)


def conv_kernel(slots, count, rows, history, taps, bias, mix_weight, *rest):
    pieces, (out, out_mix, weight, sems) = rest[:count], rest[count:]

    @pl.when(pl.program_id(0) == 0)
    def _():
        for copy in load_rows(pieces, weight, sems, row_starts(pieces)):
            copy.wait()

    made = jnp.dot(rows[...], weight[...], preferred_element_type=jnp.float32)
    steps = made.shape[0] // slots
    tap_count = taps.shape[0]
    past = history.shape[1]
    sequence = [
        jnp.broadcast_to(history[0, index : index + 1, :], (slots, made.shape[1]))
        for index in range(past)
    ] + [made[step * slots : (step + 1) * slots] for step in range(steps)]
    for step in range(steps):
        value = bias[...]
        for tap in range(tap_count):
            value = value + taps[tap : tap + 1, :] * sequence[step + tap]
        out[step * slots : (step + 1) * slots, :] = jax.nn.silu(value).astype(jnp.bfloat16)
    out_mix[...] = jnp.dot(
        out[...], mix_weight[...], preferred_element_type=jnp.float32
    ).astype(jnp.bfloat16)


def scan_kernel(
    slots,
    conv,
    mix_own,
    mix_other,
    step_weight,
    step_bias,
    decay_log,
    skip,
    state,
    out,
    step_scratch,
    drive_scratch,
    out_scratch,
    rate_scratch,
    state_scratch,
    in_scratch,
    out_mix_scratch,
):
    lanes = 128
    rank = step_weight.shape[0]
    states, channels = decay_log.shape
    total_rows = conv.shape[0]
    steps = total_rows // slots
    block = 8
    mix = mix_own[...].astype(jnp.float32) + mix_other[...].astype(jnp.float32)
    raw = (
        jnp.dot(
            mix[:, :rank].astype(jnp.bfloat16), step_weight[...], preferred_element_type=jnp.float32
        )
        + step_bias[...]
    )
    step = jax.nn.softplus(raw)
    value = conv[...].astype(jnp.float32)
    step_scratch[:, :channels] = step
    drive_scratch[:, :channels] = step * value
    rate_scratch[:, :channels] = -jnp.exp(decay_log[...]) * LOG2_E
    state_scratch[:, :channels] = state[0]
    for n in range(states):
        in_scratch[n] = jnp.broadcast_to(mix[:, rank + n : rank + n + 1], (total_rows, lanes))
        out_mix_scratch[n] = jnp.broadcast_to(
            mix[:, rank + states + n : rank + states + n + 1], (total_rows, lanes)
        )
    chunks = step_scratch.shape[1] // lanes

    def one(index, carry):
        chunk = index // (slots // block)
        part = index % (slots // block)
        columns = pl.ds(pl.multiple_of(chunk * lanes, lanes), lanes)
        held = [
            jnp.broadcast_to(state_scratch[n : n + 1, columns], (block, lanes))
            for n in range(states)
        ]
        for t in range(steps):
            where = pl.ds(pl.multiple_of(t * slots + part * block, block), block)
            size = step_scratch[where, columns]
            drive = drive_scratch[where, columns]
            total = None
            for n in range(states):
                rate = jnp.broadcast_to(rate_scratch[n : n + 1, columns], (block, lanes))
                held[n] = jnp.exp2(size * rate) * held[n] + drive * in_scratch[n, where, :]
                term = held[n] * out_mix_scratch[n, where, :]
                total = term if total is None else total + term
            out_scratch[where, columns] = total
        return carry

    lax.fori_loop(0, chunks * (slots // block), one, 0)
    out[...] = out_scratch[:, :channels] + skip[...] * value


def branch_kernel(gate_count, ssm_count, attn_count, half_start, rows, scanned, heads, *rest):
    gate_pieces = rest[:gate_count]
    ssm_pieces = rest[gate_count : gate_count + ssm_count]
    attn_pieces = rest[gate_count + ssm_count : gate_count + ssm_count + attn_count]
    (
        keep_ssm,
        send_ssm,
        keep_attn,
        send_attn,
        gate_weight,
        ssm_weight,
        attn_weight,
        gate_sems,
        ssm_sems,
        attn_sems,
    ) = rest[gate_count + ssm_count + attn_count :]
    width = ssm_weight.shape[0]
    half = width // 2

    def starts(pieces):
        first = half_start[0] * half
        return [
            pl.multiple_of(start + first if start < half else start - first, 16)
            for start in row_starts(pieces)
        ]

    @pl.when(pl.program_id(0) == 0)
    def _():
        copies = load_rows(gate_pieces, gate_weight, gate_sems, row_starts(gate_pieces))
        copies += load_rows(ssm_pieces, ssm_weight, ssm_sems, starts(ssm_pieces))
        copies += load_rows(attn_pieces, attn_weight, attn_sems, starts(attn_pieces))
        for copy in copies:
            copy.wait()

    gate = jnp.dot(rows[...], gate_weight[...], preferred_element_type=jnp.float32)
    gated = (scanned[...] * jax.nn.silu(gate)).astype(jnp.bfloat16)
    attended = heads[...]
    contract = (((1,), (1,)), ((), ()))

    def product(left, right):
        return lax.dot_general(left, right, contract, preferred_element_type=jnp.float32).astype(
            jnp.bfloat16
        )

    send_ssm[...] = product(gated, ssm_weight[half:, :])
    keep_ssm[...] = product(gated, ssm_weight[:half, :])
    send_attn[...] = product(attended, attn_weight[half:, :])
    keep_attn[...] = product(attended, attn_weight[:half, :])


def square_kernel(keep_ssm, got_ssm, keep_attn, got_attn, out):
    ssm = keep_ssm[...].astype(jnp.float32) + got_ssm[...].astype(jnp.float32)
    attn = keep_attn[...].astype(jnp.float32) + got_attn[...].astype(jnp.float32)
    out[:, 0:1] = jnp.sum(attn * attn, axis=1, keepdims=True)
    out[:, 1:2] = jnp.sum(ssm * ssm, axis=1, keepdims=True)


def mixed_kernel(
    slots,
    places,
    sizes,
    x_rows,
    keep_ssm,
    got_ssm,
    keep_attn,
    got_attn,
    squares,
    attn_gain,
    ssm_gain,
    features,
    out,
):
    group = pl.program_id(0)
    ssm = keep_ssm[...].astype(jnp.float32) + got_ssm[...].astype(jnp.float32)
    attn = keep_attn[...].astype(jnp.float32) + got_attn[...].astype(jnp.float32)
    scales = lax.rsqrt(squares[...] / D + EPSILON)
    branch = 0.5 * (
        attn_gain[...] * attn * scales[:, 0:1] + ssm_gain[...] * ssm * scales[:, 1:2]
    )
    mixed = x_rows[...].astype(jnp.float32) + branch
    count = mixed.shape[0]
    slot = lax.broadcasted_iota(jnp.int32, (count, 1), 0) % slots
    mixed = jnp.where(slot < sizes[group], mixed, 0.0).astype(jnp.bfloat16)
    steps = count // slots
    to_row = lax.broadcasted_iota(jnp.int32, (count, count), 0)
    from_row = lax.broadcasted_iota(jnp.int32, (count, count), 1)
    mover = jnp.where(
        from_row == (to_row % steps) * slots + to_row // steps, 1.0, 0.0
    ).astype(jnp.bfloat16)
    placed = jnp.dot(mixed, features[...], preferred_element_type=jnp.float32).astype(jnp.bfloat16)
    out[0] = jnp.dot(mover, placed, preferred_element_type=jnp.float32).astype(jnp.bfloat16)


def local(
    tokens,
    prefix_kv,
    ssm_state,
    conv_state,
    prefix_len,
    group_size,
    serve_replica,
    in_gain,
    w_query,
    w_keyval,
    w_inner,
    conv_weight,
    conv_bias,
    w_xproj,
    dt_weight,
    dt_bias,
    decay_log,
    skip_gain,
    w_attn_out,
    w_ssm_out,
    attn_gain,
    ssm_gain,
):
    rep_count = lax.axis_size("rep")
    row_axis = lax.axis_size("tr")
    tensor_count = lax.axis_size("tc")
    rep = lax.axis_index("rep")
    row = lax.axis_index("tr")
    core = lax.axis_index("tc")
    groups, slots, steps, width = tokens.shape
    pairs = groups // rep_count
    kv_here = KVH // tensor_count
    per_kv = QH // KVH
    heads_width = QH // tensor_count * HD
    group_rows = slots * steps
    rows = groups * group_rows
    channels = w_inner.shape[2]
    shards = rep_count * row_axis
    shard = w_query.shape[0]
    pad = -(-shard // 8) * 8
    depth = shards * pad
    half = depth // 2
    by_links = rep_count == 4 and row_axis == 4
    bf16 = jnp.bfloat16
    f32 = jnp.float32

    def padded(value):
        return jnp.pad(value, ((0, pad - shard), (0, 0)))

    gate_shard = padded(w_inner[:, 1])
    qkv_shard = padded(jnp.concatenate([w_query, w_keyval], axis=1))
    conv_shard = padded(w_inner[:, 0])
    out_shard = padded(jnp.concatenate([w_attn_out.T, w_ssm_out.T], axis=1))

    slot_table = jnp.asarray(Z_SLOTS, jnp.int32)
    block_ids = jnp.arange(shards, dtype=jnp.int32)
    if by_links:
        order = jnp.sum(
            jnp.where(jnp.arange(4)[:, None] == row, slot_table, 0), axis=0
        )
        reps_here = jnp.arange(rep_count, dtype=jnp.int32) ^ rep
        pieces_a = (reps_here[:, None] * row_axis + order[None, :]).reshape(shards)
        pieces_b = (reps_here[None, :] * row_axis + order[:, None]).reshape(shards)
        second = (rep // 2) ^ core
    else:
        pieces_a = block_ids
        pieces_b = block_ids
        second = core

    def sources(pieces):
        offset = jnp.arange(pad, dtype=jnp.int32)
        return jnp.where(offset < shard, pieces[:, None] * shard + offset, -1).reshape(depth)

    source_a = sources(pieces_a)
    source_b = sources(pieces_b)
    keep_source = lax.dynamic_slice_in_dim(source_a, second * half, half, 0)
    own_features = core * width + jnp.arange(width, dtype=jnp.int32)
    other_features = (1 - core) * width + jnp.arange(width, dtype=jnp.int32)

    def pick(features, source):
        return (features[:, None] == source[None, :]).astype(bf16)

    spread_keep = pick(own_features, keep_source)
    features_keep = (keep_source[:, None] == own_features[None, :]).astype(bf16)

    def gain_columns(gain):
        matches = keep_source[:, None] == jnp.arange(gain.shape[0], dtype=jnp.int32)[None, :]
        return jnp.sum(jnp.where(matches, gain[None, :], 0.0), axis=1)[None, :]

    attn_gain_here = gain_columns(attn_gain)
    ssm_gain_here = gain_columns(ssm_gain)

    first_group = (rep * row_axis + row) * groups
    lengths = lax.dynamic_slice_in_dim(prefix_len, first_group, groups, 0)
    sizes = lax.dynamic_slice_in_dim(group_size, first_group, groups, 0)
    served = lax.dynamic_slice_in_dim(serve_replica, first_group, groups, 0)
    target = served ^ rep if by_links else served
    same = (served[:, None] == served[None, :]) & (
        jnp.arange(groups)[None, :] < jnp.arange(groups)[:, None]
    )
    places = (target * pairs + jnp.sum(same.astype(jnp.int32), axis=1)).astype(jnp.int32)

    x_bf = tokens.transpose(0, 2, 1, 3).reshape(rows, width)
    x_rows = x_bf.astype(f32)
    square_sums = lax.psum(jnp.sum(x_rows * x_rows, axis=1), "tc")
    inv_rms = lax.rsqrt(square_sums / D + EPSILON)
    normed_own = (x_rows * inv_rms[:, None] * in_gain[None, :]).astype(bf16)
    normed_other = other_core(normed_own)

    def row_block(columns):
        return pl.BlockSpec((group_rows, columns), lambda g, *_: (g, 0))

    def whole(*shape):
        return pl.BlockSpec(shape, lambda g, *_: (0,) * len(shape))

    anywhere = pl.BlockSpec(memory_space=pl.ANY)

    rows_a, rows_b, x_keep = pl.pallas_call(
        spread_kernel,
        grid=(groups,),
        in_specs=[row_block(width)] * 3 + [whole(width, depth)] * 4 + [whole(width, half)],
        out_specs=[row_block(depth), row_block(depth), row_block(half)],
        out_shape=[
            jax.ShapeDtypeStruct((rows, depth), bf16),
            jax.ShapeDtypeStruct((rows, depth), bf16),
            jax.ShapeDtypeStruct((rows, half), bf16),
        ],
        compiler_params=params(),
        cost_estimate=cost(2 * rows * depth * D * 3, rows * D * 10),
        name="spread_rows",
    )(
        normed_own,
        normed_other,
        x_bf,
        pick(own_features, source_a),
        pick(other_features, source_a),
        pick(own_features, source_b),
        pick(other_features, source_b),
        spread_keep,
    )

    def attention(pieces):
        return pl.pallas_call(
            functools.partial(attention_kernel, slots, kv_here, per_kv, len(pieces)),
            grid_spec=pltpu.PrefetchScalarGridSpec(
                num_scalar_prefetch=1,
                grid=(groups,),
                in_specs=[
                    row_block(depth),
                    pl.BlockSpec((1,) + prefix_kv.shape[1:], lambda g, *_: (g, 0, 0)),
                ]
                + [anywhere] * len(pieces),
                out_specs=row_block(heads_width),
                scratch_shapes=[
                    pltpu.VMEM((depth, pieces[0].shape[1]), bf16),
                    pltpu.SemaphoreType.DMA((len(pieces),)),
                ],
            ),
            out_shape=jax.ShapeDtypeStruct((rows, heads_width), bf16),
            compiler_params=params(),
            cost_estimate=cost(2 * rows * depth * 768 * 4, rows * depth * 2),
            name="attention",
        )(lengths, rows_a, prefix_kv, *pieces)

    def convolve(pieces):
        mixes = w_xproj.shape[1]
        return pl.pallas_call(
            functools.partial(conv_kernel, slots, len(pieces)),
            grid=(groups,),
            in_specs=[
                row_block(depth),
                pl.BlockSpec((1,) + conv_state.shape[1:], lambda g: (g, 0, 0)),
                whole(*conv_weight.shape),
                whole(1, channels),
                whole(*w_xproj.shape),
            ]
            + [anywhere] * len(pieces),
            out_specs=[row_block(channels), row_block(mixes)],
            out_shape=[
                jax.ShapeDtypeStruct((rows, channels), bf16),
                jax.ShapeDtypeStruct((rows, mixes), bf16),
            ],
            scratch_shapes=[
                pltpu.VMEM((depth, channels), bf16),
                pltpu.SemaphoreType.DMA((len(pieces),)),
            ],
            compiler_params=params(),
            cost_estimate=cost(2 * rows * depth * channels * 1.5, rows * depth * 4),
            name="convolve",
        )(rows_a, conv_state, conv_weight, conv_bias[None], w_xproj, *pieces)

    def scan(conv_out, mix_own, mix_other):
        rank, states = dt_weight.shape[0], decay_log.shape[0]
        wide = -(-channels // 128) * 128
        mixes = w_xproj.shape[1]
        return pl.pallas_call(
            functools.partial(scan_kernel, slots),
            grid=(groups,),
            in_specs=[
                row_block(channels),
                row_block(mixes),
                row_block(mixes),
                whole(rank, channels),
                whole(1, channels),
                whole(states, channels),
                whole(1, channels),
                pl.BlockSpec((1,) + ssm_state.shape[1:], lambda g: (g, 0, 0)),
            ],
            out_specs=row_block(channels),
            out_shape=jax.ShapeDtypeStruct((rows, channels), f32),
            scratch_shapes=[
                pltpu.VMEM((group_rows, wide), f32),
                pltpu.VMEM((group_rows, wide), f32),
                pltpu.VMEM((group_rows, wide), f32),
                pltpu.VMEM((states, wide), f32),
                pltpu.VMEM((states, wide), f32),
                pltpu.VMEM((states, group_rows, 128), f32),
                pltpu.VMEM((states, group_rows, 128), f32),
            ],
            compiler_params=params(),
            cost_estimate=cost(30e-6 * 1.1e15, rows * channels * 6),
            name="scan_states",
        )(
            conv_out,
            mix_own,
            mix_other,
            dt_weight,
            dt_bias[None],
            decay_log,
            skip_gain[None],
            ssm_state,
        )

    def branches(scanned, heads, gate_pieces, ssm_pieces, attn_pieces):
        return pl.pallas_call(
            functools.partial(
                branch_kernel, len(gate_pieces), len(ssm_pieces), len(attn_pieces)
            ),
            grid_spec=pltpu.PrefetchScalarGridSpec(
                num_scalar_prefetch=1,
                grid=(groups,),
                in_specs=[row_block(depth), row_block(channels), row_block(heads_width)]
                + [anywhere] * (len(gate_pieces) + len(ssm_pieces) + len(attn_pieces)),
                out_specs=[row_block(half)] * 4,
                scratch_shapes=[
                    pltpu.VMEM((depth, channels), bf16),
                    pltpu.VMEM((depth, channels), bf16),
                    pltpu.VMEM((depth, heads_width), bf16),
                    pltpu.SemaphoreType.DMA((len(gate_pieces),)),
                    pltpu.SemaphoreType.DMA((len(ssm_pieces),)),
                    pltpu.SemaphoreType.DMA((len(attn_pieces),)),
                ],
            ),
            out_shape=[jax.ShapeDtypeStruct((rows, half), bf16)] * 4,
            compiler_params=params(),
            cost_estimate=cost(2 * rows * depth * channels * 2.5, rows * depth * 8),
            name="branches",
        )(second.astype(jnp.int32)[None], rows_b, scanned, heads, *gate_pieces, *ssm_pieces, *attn_pieces)

    if by_links:
        def line_first(value):
            return along_z(value, Z_OUTER), along_z(value, Z_INNER)

        def line_second(near, middle):
            return along_z(near, Z_INNER), along_z(middle, Z_ENDS), along_z(near, Z_FAR)

        inner = (row == 1) | (row == 2)

        def line_slots(value, first, last):
            near, middle = first
            crossed, ends, far = last
            return value, near, jnp.where(inner, middle, ends), jnp.where(inner, crossed, far)

        def plane_first(value):
            return swap_x(value), swap_y(value)

        def plane_second(first):
            by_x, by_y = first
            cut = by_x.shape[0] // 16 * 8
            return swap_y(by_x[:cut]), swap_x(by_y[cut:])

        gate_p1 = plane_first(gate_shard)
        qkv_z1 = line_first(qkv_shard)
        conv_z1 = line_first(conv_shard)

        gate_p1 = after(gate_p1, qkv_z1 + conv_z1)
        gate_p2 = plane_second(gate_p1)
        qkv_z2 = line_second(*after(qkv_z1, gate_p1))

        gate_block = jnp.concatenate((gate_shard,) + tuple(gate_p1) + tuple(gate_p2), axis=0)
        qkv_block = jnp.concatenate(line_slots(qkv_shard, qkv_z1, qkv_z2), axis=0)
        qkv_p1 = plane_first(qkv_block)
        conv_z2 = line_second(*after(conv_z1, (qkv_block,)))

        conv_block = jnp.concatenate(line_slots(conv_shard, conv_z1, conv_z2), axis=0)
        qkv_p1 = after(qkv_p1, (conv_block,))
        qkv_p2 = plane_second(qkv_p1)
        out_z1 = line_first(*after((out_shard,), (conv_block,)))

        (conv_block,) = after((conv_block,), qkv_p2 + out_z1)
        conv_p1 = plane_first(conv_block)
        (gate_block,) = after((gate_block,), (conv_block,))
        gate_z1 = line_first(gate_block)
        heads = attention((qkv_block,) + tuple(qkv_p1) + tuple(qkv_p2))

        conv_p1 = after(conv_p1, gate_z1)
        conv_p2 = plane_second(conv_p1)
        out_z2 = line_second(*after(out_z1, gate_z1))

        out_block = jnp.concatenate(line_slots(out_shard, out_z1, out_z2), axis=0)
        (out_block,) = after((out_block,), conv_p2)
        out_p1 = plane_first(out_block)
        gate_z2 = line_second(*after(gate_z1, (out_block,)))
        conv_out, mix_own = convolve((conv_block,) + tuple(conv_p1) + tuple(conv_p2))
        scanned = scan(conv_out, mix_own, other_core(mix_own))
        out_p2 = plane_second(out_p1)
        out_pieces = (out_block,) + tuple(out_p1) + tuple(out_p2)
        gate_pieces = line_slots(gate_block, gate_z1, gate_z2)
        attn_pieces = [piece[:, :heads_width] for piece in out_pieces]
        ssm_pieces = [piece[:, heads_width:] for piece in out_pieces]
    else:
        def gathered(value):
            return lax.all_gather(value, ("rep", "tr"), axis=0, tiled=True)

        heads = attention((gathered(qkv_shard),))
        conv_out, mix_own = convolve((gathered(conv_shard),))
        scanned = scan(conv_out, mix_own, other_core(mix_own))
        out_all = gathered(out_shard)
        gate_pieces = (gathered(gate_shard),)
        attn_pieces = [out_all[:half, :heads_width], out_all[half:, :heads_width]]
        ssm_pieces = [out_all[:half, heads_width:], out_all[half:, heads_width:]]

    keep_ssm, send_ssm, keep_attn, send_attn = branches(
        scanned, heads, gate_pieces, ssm_pieces, attn_pieces
    )
    got_ssm = other_core(send_ssm)
    got_attn = other_core(send_attn)
    squares = pl.pallas_call(
        square_kernel,
        grid=(groups,),
        in_specs=[row_block(half)] * 4,
        out_specs=row_block(2),
        out_shape=jax.ShapeDtypeStruct((rows, 2), f32),
        compiler_params=params(),
        cost_estimate=cost(rows * half * 8, rows * half * 8),
        name="squares",
    )(keep_ssm, got_ssm, keep_attn, got_attn)
    squares = squares + other_core(squares)
    mixed = pl.pallas_call(
        functools.partial(mixed_kernel, slots),
        grid_spec=pltpu.PrefetchScalarGridSpec(
            num_scalar_prefetch=2,
            grid=(groups,),
            in_specs=[row_block(half)] * 5
            + [row_block(2), whole(1, half), whole(1, half), whole(half, width)],
            out_specs=pl.BlockSpec(
                (1, group_rows, width), lambda g, places, sizes: (places[g], 0, 0)
            ),
        ),
        out_shape=jax.ShapeDtypeStruct((groups, group_rows, width), bf16),
        compiler_params=params(),
        cost_estimate=cost(2 * rows * half * width, rows * half * 12),
        name="mixed_rows",
    )(
        places,
        sizes,
        x_keep,
        keep_ssm,
        got_ssm,
        keep_attn,
        got_attn,
        squares,
        attn_gain_here,
        ssm_gain_here,
        features_keep,
    )
    if by_links:
        parts = mixed.reshape(rep_count, pairs, group_rows, width)
        received = jnp.stack(
            [
                parts[0],
                swap_x(parts[1]),
                swap_y(parts[2]),
                lax.ppermute(parts[3], "rep", D_PAIRS),
            ]
        )
        mixed = jnp.take(received, jnp.arange(rep_count, dtype=jnp.int32) ^ rep, axis=0)
    else:
        mixed = lax.all_to_all(mixed, "rep", split_axis=0, concat_axis=0, tiled=True)
    return mixed.reshape(groups, slots, steps, width)


def solution(mesh):
    placed = (
        P(("rep", "tr"), None, None, "tc"),
        P(("rep", "tr"), None, "tc"),
        P(("rep", "tr"), None, "tc"),
        P(("rep", "tr"), None, "tc"),
        P(),
        P(),
        P(),
        P("tc"),
        P(("rep", "tr"), "tc"),
        P(("rep", "tr"), "tc"),
        P(("rep", "tr"), None, "tc"),
        P(None, "tc"),
        P("tc"),
        P("tc", None),
        P(None, "tc"),
        P("tc"),
        P(None, "tc"),
        P("tc"),
        P("tc", ("rep", "tr")),
        P("tc", ("rep", "tr")),
        P(),
        P(),
    )
    return jax.shard_map(
        local,
        mesh=mesh,
        in_specs=placed,
        out_specs=P(("rep", "tr"), None, None, "tc"),
        check_vma=False,
    )
```

```python
import functools

import jax
import jax.numpy as jnp
from jax import lax
from jax.experimental import pallas as pl
from jax.experimental.pallas import tpu as pltpu
from jax.sharding import PartitionSpec as P

D = 1600
HD = 64
QH = 16
KVH = 4

EPSILON = 1e-06
LOG2_E = 1.4426950408889634

X_PAIRS = ((0, 1), (1, 0), (2, 3), (3, 2))
Y_PAIRS = ((0, 2), (2, 0), (1, 3), (3, 1))
D_PAIRS = ((0, 3), (3, 0), (1, 2), (2, 1))
Z_OUTER = ((0, 1), (1, 0), (2, 3), (3, 2))
Z_INNER = ((1, 2), (2, 1))
Z_ENDS = ((1, 0), (2, 3))
Z_FAR = ((2, 0), (1, 3))
Z_SLOTS = ((0, 1, 2, 3), (1, 0, 2, 3), (2, 3, 1, 0), (3, 2, 1, 0))

VMEM_LIMIT = 56 * 1024 * 1024


def params():
    return pltpu.CompilerParams(vmem_limit_bytes=VMEM_LIMIT)


def cost(flops, size):
    return pl.CostEstimate(flops=int(flops), bytes_accessed=int(size), transcendentals=0)


def tie(*values):
    return lax.optimization_barrier(values)


def swap_x(value):
    return lax.ppermute(value, "rep", X_PAIRS)


def swap_y(value):
    return lax.ppermute(value, "rep", Y_PAIRS)


def along_z(value, pairs):
    return lax.ppermute(value, "tr", pairs)


def other_core(value):
    return lax.ppermute(value, "tc", ((0, 1), (1, 0)))


def load_halves(pieces, target, sems, second, half, wide, column=0):
    width = target.shape[1]
    if wide > half:
        gap = jnp.zeros((wide - half, width), target.dtype)
        target[half:wide, :] = gap
        target[wide + half :, :] = gap
    copies = []
    start = 0
    for piece in pieces:
        count = piece.shape[0]
        for low in range(0, count, half):
            size = min(half, count)
            at_first = start < half
            place = (second if at_first else 1 - second) * wide + start % half
            copies.append(
                pltpu.make_async_copy(
                    piece.at[pl.ds(low, size), pl.ds(column, width)],
                    target.at[pl.ds(pl.multiple_of(place, 16), size), :],
                    sems.at[len(copies)],
                )
            )
            start += size
    for copy in copies:
        copy.start()
    for copy in copies:
        copy.wait()


def silu(value):
    scaled = 0.5 * value
    return scaled + scaled * jnp.tanh(scaled)


def row_mover(slots, steps, inward):
    count = slots * steps
    to_row = lax.broadcasted_iota(jnp.int32, (count, count), 0)
    from_row = lax.broadcasted_iota(jnp.int32, (count, count), 1)
    if inward:
        source = (to_row % slots) * steps + to_row // slots
    else:
        source = (to_row % steps) * slots + to_row // steps
    return jnp.where(from_row == source, 1.0, 0.0).astype(jnp.bfloat16)


def both_halves(rows_own, rows_other, weight):
    rows = jnp.concatenate([rows_own[...], rows_other[...]], axis=1)
    return jnp.dot(rows, weight[...], preferred_element_type=jnp.float32)


def exact_dot(left, right):
    return jnp.dot(left, right, preferred_element_type=jnp.float32).astype(jnp.bfloat16)


def spread_kernel(slots, proc, x, inv_rms, gain, pick, out):
    normed = (x[0].astype(jnp.float32) * inv_rms[0] * gain[...]).astype(jnp.bfloat16)
    mover = row_mover(slots, x.shape[1] // slots, True)
    out[...] = exact_dot(exact_dot(mover, normed), pick[...])


def place_kernel(slots, proc, x, pick, out):
    mover = row_mover(slots, x.shape[1] // slots, True)
    out[...] = exact_dot(exact_dot(mover, x[0]), pick[...])


def attention_kernel(
    slots,
    group_rows,
    kv_here,
    per_kv,
    count,
    half,
    first_column,
    proc,
    lengths,
    second,
    rows_own,
    rows_other,
    cache,
    *rest,
):
    pieces, (out, weight, sems) = rest[:count], rest[count:]
    tile = pl.program_id(0)

    @pl.when(tile == 0)
    def _():
        load_halves(pieces, weight, sems, second[0], half, weight.shape[0] // 2, first_column)

    made = both_halves(rows_own, rows_other, weight).astype(jnp.bfloat16)
    here = made.shape[0] // group_rows
    query_width = kv_here * per_kv * HD
    positions = cache.shape[1]
    stacked = per_kv * group_rows
    row_id = lax.broadcasted_iota(jnp.int32, (stacked, group_rows), 0) % group_rows
    column_id = lax.broadcasted_iota(jnp.int32, (stacked, group_rows), 1)
    own_mask = (row_id % slots == column_id % slots) & (column_id // slots <= row_id // slots)
    column = lax.broadcasted_iota(jnp.int32, (stacked, positions), 1)
    contract = (((1,), (1,)), ((), ()))
    scale = HD ** (-0.5)
    for index in range(here):
        group = proc[tile * here + index]
        prefix_mask = column < lengths[group]
        block = made[index * group_rows : (index + 1) * group_rows]
        past = cache[group]
        results = []
        for head in range(kv_here):
            query = jnp.concatenate(
                [
                    block[:, (head * per_kv + j) * HD : (head * per_kv + j + 1) * HD]
                    for j in range(per_kv)
                ],
                axis=0,
            )
            base = query_width + head * 2 * HD
            key_new = block[:, base : base + HD]
            value_new = block[:, base + HD : base + 2 * HD]
            key_old = past[:, head * 2 * HD : head * 2 * HD + HD]
            value_old = past[:, head * 2 * HD + HD : (head + 1) * 2 * HD]
            old = lax.dot_general(query, key_old, contract, preferred_element_type=jnp.float32)
            new = lax.dot_general(query, key_new, contract, preferred_element_type=jnp.float32)
            old = jnp.where(prefix_mask, old * scale, -jnp.inf)
            new = jnp.where(own_mask, new * scale, -jnp.inf)
            top = jnp.maximum(
                jnp.max(old, axis=1, keepdims=True), jnp.max(new, axis=1, keepdims=True)
            )
            old = jnp.exp(old - top)
            new = jnp.exp(new - top)
            total = jnp.sum(old, axis=1, keepdims=True) + jnp.sum(new, axis=1, keepdims=True)
            value = jnp.dot(
                old.astype(jnp.bfloat16), value_old, preferred_element_type=jnp.float32
            ) + jnp.dot(new.astype(jnp.bfloat16), value_new, preferred_element_type=jnp.float32)
            value = (value / total).astype(jnp.bfloat16)
            for j in range(per_kv):
                results.append(value[j * group_rows : (j + 1) * group_rows])
        out[index * group_rows : (index + 1) * group_rows, :] = jnp.concatenate(results, axis=1)


def conv_kernel(
    slots,
    group_rows,
    count,
    half,
    first_column,
    proc,
    second,
    rows_own,
    rows_other,
    history,
    taps,
    bias,
    mix_weight,
    *rest,
):
    pieces, (out, out_mix, weight, sems) = rest[:count], rest[count:]
    tile = pl.program_id(0)

    @pl.when(tile == 0)
    def _():
        load_halves(pieces, weight, sems, second[0], half, weight.shape[0] // 2, first_column)

    made = both_halves(rows_own, rows_other, weight)
    here = made.shape[0] // group_rows
    steps = group_rows // slots
    tap_count = taps.shape[0]
    past = history.shape[1]
    for index in range(here):
        start = index * group_rows
        state = history[proc[tile * here + index]]
        sequence = [
            jnp.broadcast_to(state[k : k + 1, :], (slots, made.shape[1])) for k in range(past)
        ] + [made[start + step * slots : start + (step + 1) * slots] for step in range(steps)]
        for step in range(steps):
            value = bias[...]
            for tap in range(tap_count):
                value = value + taps[tap : tap + 1, :] * sequence[step + tap]
            out[start + step * slots : start + (step + 1) * slots, :] = silu(value).astype(
                jnp.bfloat16
            )
    out_mix[...] = jnp.dot(
        out[...], mix_weight[...], preferred_element_type=jnp.float32
    ).astype(jnp.bfloat16)


def softplus(value):
    small = jnp.exp(-jnp.abs(value))
    series = small * (1.0 - small * (0.5 - small * (1.0 / 3.0)))
    return jnp.maximum(value, 0.0) + jnp.where(small < 0.01, series, jnp.log(1.0 + small))


def scan_kernel(
    slots, proc, conv, mix_own, mix_other, step_weight, step_bias, decay_log, skip, state, *rest
):
    out, *scratch = rest[-8:]
    step_scratch, drive_scratch, out_scratch, rate_scratch, state_scratch, in_mix, out_mix = scratch
    lanes = 128
    kind = jnp.bfloat16
    rank = step_weight.shape[0]
    states, channels = decay_log.shape
    total_rows = conv.shape[0]
    mix = mix_own[...].astype(jnp.float32) + mix_other[...].astype(jnp.float32)
    raw = (
        jnp.dot(mix[:, :rank].astype(kind), step_weight[...], preferred_element_type=jnp.float32)
        + step_bias[...]
    )
    step = softplus(raw)
    value = conv[...].astype(jnp.float32)
    step_scratch[:, :channels] = step
    drive_scratch[:, :channels] = step * value
    rate_scratch[:, :channels] = -jnp.exp(decay_log[...]) * LOG2_E
    state_scratch[:, :channels] = state[0]
    for n in range(states):
        in_mix[n] = jnp.broadcast_to(mix[:, 128 + n : 129 + n], (total_rows, lanes)).astype(kind)
        out_mix[n] = jnp.broadcast_to(
            mix[:, 128 + states + n : 129 + states + n], (total_rows, lanes)
        ).astype(kind)

    def one(chunk, carry):
        columns = pl.ds(pl.multiple_of(chunk * lanes, lanes), lanes)

        def spread(source, n):
            return jnp.broadcast_to(source[n : n + 1, columns], (slots, lanes)).astype(kind)

        held = [spread(state_scratch, n) for n in range(states)]
        for start in range(0, total_rows, slots):
            here = pl.ds(start, slots)
            size = step_scratch[here, columns].astype(kind)
            drive = drive_scratch[here, columns].astype(kind)
            total = None
            for first in range(0, states, 4):
                part = None
                for n in range(first, first + 4):
                    held[n] = jnp.exp2(size * spread(rate_scratch, n)) * held[n] + drive * in_mix[n, here, :]
                    term = held[n] * out_mix[n, here, :]
                    part = term if part is None else part + term
                part = part.astype(jnp.float32)
                total = part if total is None else total + part
            out_scratch[here, columns] = total
        return carry

    lax.fori_loop(0, step_scratch.shape[1] // lanes, one, 0)
    out[...] = out_scratch[:, :channels] + skip[...] * value


def gate_kernel(count, half, first_column, second, rows_own, rows_other, scanned, *rest):
    pieces, (out, weight, sems) = rest[:count], rest[count:]

    @pl.when(pl.program_id(0) == 0)
    def _():
        load_halves(pieces, weight, sems, second[0], half, weight.shape[0] // 2, first_column)

    gate = both_halves(rows_own, rows_other, weight)
    out[...] = (scanned[...] * silu(gate)).astype(jnp.bfloat16)


def transposed_dot(left, right):
    return lax.dot_general(
        left, right, (((1,), (1,)), ((), ())), preferred_element_type=jnp.float32
    ).astype(jnp.bfloat16)


def attn_out_kernel(count, half, first_column, blocks, second, heads, *rest):
    pieces, (keep, send, raw, weight, sems) = rest[:count], rest[count:]
    wide = raw.shape[0] // 2
    columns = weight.shape[0] // 2

    @pl.when(pl.program_id(0) == 0)
    def _():
        load_halves(pieces, raw, sems, second[0], half, wide, first_column)
        loaded = raw[...].astype(jnp.float32)
        for index in range(2):
            parts = [
                jnp.zeros((size, loaded.shape[1]), jnp.float32)
                if at is None
                else loaded[index * wide + at : index * wide + at + size]
                for at, size in blocks
            ]
            weight[index * columns : (index + 1) * columns, :] = jnp.concatenate(
                parts, axis=0
            ).astype(weight.dtype)

    attended = heads[...]
    keep[...] = transposed_dot(attended, weight[:columns, :])
    send[...] = transposed_dot(attended, weight[columns:, :])


def ssm_out_kernel(slot_choices, part, summed, scalars, gated, *rest):
    ready, rest = rest[:summed], rest[summed:]
    count = sum(slot_choices)
    pieces, (keep, send, *sums, weight, sems) = rest[:count], rest[count:]
    wide = weight.shape[0] // 2
    filled = part * len(slot_choices)
    second = scalars[0]

    @pl.when(pl.program_id(0) == 0)
    def _():
        if wide > filled:
            gap = jnp.zeros((wide - filled, weight.shape[1]), weight.dtype)
            weight[filled:wide, :] = gap
            weight[wide + filled :, :] = gap

        def copies(source, slot):
            for index, base in ((0, second), (1, 1 - second)):
                yield pltpu.make_async_copy(
                    source.at[pl.ds(pl.multiple_of(base * part, 16), part), :],
                    weight.at[pl.ds(index * wide + slot * part, part), :],
                    sems.at[slot, index],
                )

        at = 0
        firsts = []
        for slot, choices in enumerate(slot_choices):
            firsts.append(pieces[at])
            if choices == 1:
                for copy in copies(pieces[at], slot):
                    copy.start()
            else:
                for choice in range(2):

                    @pl.when(scalars[1] == 1 - choice)
                    def _(piece=pieces[at + choice], slot=slot):
                        for copy in copies(piece, slot):
                            copy.start()

            at += choices
        for slot, piece in enumerate(firsts):
            for copy in copies(piece, slot):
                copy.wait()

    value = gated[...]
    send[...] = transposed_dot(value, weight[wide:, :])
    keep[...] = transposed_dot(value, weight[:wide, :])
    if ready:
        sums[0][:, 0:1] = square_sum(ready[0], ready[1])
        sums[0][:, 1:2] = square_sum(ready[2], ready[3])


def square_sum(keep, got):
    value = keep[...].astype(jnp.float32) + got[...].astype(jnp.float32)
    return jnp.sum(value * value, axis=1, keepdims=True)


def square_kernel(*refs):
    *refs, out = refs
    if len(refs) == 4:
        out[:, 0:1] = square_sum(refs[0], refs[1])
        out[:, 1:2] = square_sum(refs[2], refs[3])
    else:
        out[:, 0:1] = refs[0][:, 0:1]
        out[:, 1:2] = refs[0][:, 1:2] + square_sum(refs[1], refs[2])


def mixed_kernel(slots, first, sections, here, proc, sizes, x_keep, keep_attn, got_attn, *rest):
    ssm_refs = rest[: 2 * sections]
    own_squares, other_squares, gains, features = rest[2 * sections : 2 * sections + 4]
    outs = rest[2 * sections + 4 : 2 * sections + 4 + here]
    made, sems = rest[2 * sections + 4 + here :]
    step = pl.program_id(0)
    ssm = jnp.concatenate(
        [
            keep[...].astype(jnp.float32) + got[...].astype(jnp.float32)
            for keep, got in zip(ssm_refs[::2], ssm_refs[1::2])
        ],
        axis=1,
    )
    attn = keep_attn[...].astype(jnp.float32) + got_attn[...].astype(jnp.float32)
    scales = lax.rsqrt((own_squares[...] + other_squares[...]) / D + EPSILON)
    branch = 0.5 * (
        gains[0:1, :] * attn * scales[:, 0:1] + gains[1:2, :] * ssm * scales[:, 1:2]
    )
    mixed = (x_keep[...].astype(jnp.float32) + branch).astype(jnp.bfloat16)
    placed = exact_dot(mixed, features[...])
    size = made.shape[1]
    in_step = mixed.shape[0] // size
    outward = row_mover(slots, size // slots, False)
    slot = lax.broadcasted_iota(jnp.int32, (size, 1), 0) // (size // slots)

    def copy(number):
        return pltpu.make_async_copy(made.at[number], outs[number], sems.at[number])

    for index in range(in_step):
        number = step * in_step + index
        rows = exact_dot(outward, placed[index * size : (index + 1) * size])
        live = slot < sizes[proc[first + number]]
        made[number] = jnp.where(live, rows, jnp.zeros_like(rows))
    for number in range(here):

        @pl.when(step == number // in_step)
        def _(number=number):
            copy(number).start()

    @pl.when(step == here // in_step - 1)
    def _():
        for number in range(here):
            copy(number).wait()


def local(
    tokens,
    prefix_kv,
    ssm_state,
    conv_state,
    prefix_len,
    group_size,
    serve_replica,
    in_gain,
    w_query,
    w_keyval,
    w_inner,
    conv_weight,
    conv_bias,
    w_xproj,
    dt_weight,
    dt_bias,
    decay_log,
    skip_gain,
    w_attn_out,
    w_ssm_out,
    attn_gain,
    ssm_gain,
):
    rep_count = lax.axis_size("rep")
    row_axis = lax.axis_size("tr")
    tensor_count = lax.axis_size("tc")
    rep = lax.axis_index("rep")
    row = lax.axis_index("tr")
    core = lax.axis_index("tc")
    groups, slots, steps, width = tokens.shape
    pairs = groups // rep_count
    kv_here = KVH // tensor_count
    per_kv = QH // KVH
    heads_width = QH // tensor_count * HD
    group_rows = slots * steps
    rows = groups * group_rows
    tile = groups // 4 * group_rows
    channels = w_inner.shape[2]
    shards = rep_count * row_axis
    shard = w_query.shape[0]
    pad = -(-shard // 8) * 8
    depth = shards * pad
    half = depth // 2
    wide = -(-half // 128) * 128
    by_links = rep_count == 4 and row_axis == 4
    sections = 2 if by_links else 1
    section = half // sections
    section_wide = -(-section // 128) * 128
    columns = sections * section_wide
    bf16 = jnp.bfloat16
    f32 = jnp.float32
    i32 = jnp.int32

    def padded(value):
        return jnp.pad(value, ((0, pad - shard), (0, 0)))

    ssm_shard = padded(w_ssm_out.T)
    conv_shard = padded(w_inner[:, 0])
    gate_shard = padded(w_inner[:, 1])
    attn_shard = padded(jnp.concatenate([w_query, w_keyval, w_attn_out.T], axis=1))
    qkv_width = w_query.shape[1] + w_keyval.shape[1]
    rank, states = dt_weight.shape[0], decay_log.shape[0]
    mixes = 256

    def feature_at(column, lines_outside, rep, row):
        inside = column < half
        if lines_outside:
            inside = column % section_wide < section
            column = column // section_wide * section + column % section_wide
        block, offset = column // pad, column % pad
        if by_links:
            if lines_outside:
                slot, plane = block // 2, block % 2
            else:
                slot, plane = block % row_axis, block // row_axis
            low = row < 2
            line = jnp.where(
                slot == 0,
                row,
                jnp.where(
                    slot == 1,
                    row ^ 1,
                    jnp.where(slot == 2, jnp.where(low, 2, 1), jnp.where(low, 3, 0)),
                ),
            )
            block = ((rep % 2) ^ plane) * row_axis + line
        return jnp.where((offset < shard) & inside, block * shard + offset, -1)

    def picker(shape, column_dim, lines_outside, rep, row):
        column = lax.broadcasted_iota(i32, shape, column_dim)
        feature = lax.broadcasted_iota(i32, shape, 1 - column_dim)
        return feature == feature_at(column, lines_outside, rep, row)

    def column_picks(rep, row):
        keep_pick = picker((width, columns), 1, True, rep, row)
        gains = jnp.stack([attn_gain, ssm_gain])
        gains = lax.dynamic_slice_in_dim(gains, core * width, width, 1)
        gains = jnp.sum(jnp.where(keep_pick[None], gains[:, :, None], 0.0), axis=1)
        features_back = picker((columns, width), 0, True, rep, row).astype(bf16)
        return keep_pick.astype(bf16), gains, features_back

    second = ((rep // 2) ^ core if by_links else core).astype(i32)[None]

    def group_order(serve_replica):
        served = lax.dynamic_slice_in_dim(serve_replica, first_group, groups, 0)
        target = served ^ rep if by_links else served
        ids = jnp.arange(groups, dtype=i32)
        same = (served[:, None] == served[None, :]) & (ids[None, :] < ids[:, None])
        places = jnp.sum(same.astype(i32), axis=1) * rep_count + target
        return jnp.sum(
            jnp.where(places[None, :] == ids[:, None], ids[None, :], 0), axis=1
        ).astype(i32)

    def inverse_rms(tokens):
        wide_rows = tokens.reshape(groups, group_rows, width).astype(f32)
        square_sums = lax.psum(jnp.sum(wide_rows * wide_rows, axis=2), "tc")
        return lax.rsqrt(square_sums / D + EPSILON)[:, :, None]

    first_group = (rep * row_axis + row) * groups
    def row_block(columns, size=tile, first=0):
        return pl.BlockSpec((size, columns), lambda g, *_: (g + first, 0))

    def whole(*shape):
        return pl.BlockSpec(shape, lambda g, *_: (0,) * len(shape))

    def group_block(*shape, first=0):
        return pl.BlockSpec(
            (1,) + shape, lambda g, proc, *_: (proc[g + first],) + (0,) * len(shape)
        )

    anywhere = pl.BlockSpec(memory_space=pl.ANY)

    def rows_of(columns, kind=bf16, count=rows):
        return jax.ShapeDtypeStruct((count, columns), kind)

    def call(kernel, scalars, grid, in_specs, out_specs, out_shape, scratch, spend, name, alias=None):
        return pl.pallas_call(
            kernel,
            grid_spec=pltpu.PrefetchScalarGridSpec(
                num_scalar_prefetch=scalars,
                grid=(grid,),
                in_specs=in_specs,
                out_specs=out_specs,
                scratch_shapes=scratch,
            ),
            out_shape=out_shape,
            input_output_aliases=alias or {},
            compiler_params=params(),
            cost_estimate=cost(spend * 1.0e7, rows * 4),
            name=name,
        )

    def piece_copies(pieces):
        return pltpu.SemaphoreType.DMA((max(len(pieces), 2),))

    def spread(inv, rep, row):
        spread_pick = picker((width, wide), 1, False, rep, row).astype(bf16)
        return call(
            functools.partial(spread_kernel, slots),
            1,
            groups,
            [
                group_block(group_rows, width),
                group_block(group_rows, 1),
                whole(1, width),
                whole(width, wide),
            ],
            row_block(wide, group_rows),
            rows_of(wide),
            [],
            8,
            "spread_rows",
        )(proc, tokens.reshape(groups, group_rows, width), inv, in_gain[None], spread_pick)

    def place(keep_pick):
        return call(
            functools.partial(place_kernel, slots),
            1,
            groups,
            [group_block(group_rows, width), whole(width, columns)],
            row_block(columns, group_rows),
            rows_of(columns),
            [],
            8,
            "place_rows",
        )(proc, tokens.reshape(groups, group_rows, width), keep_pick)

    def attention(rows_own, rows_other, pieces, lengths):
        return call(
            functools.partial(
                attention_kernel, slots, group_rows, kv_here, per_kv, len(pieces), half, 0
            ),
            3,
            rows // tile,
            [row_block(wide)] * 2 + [whole(*prefix_kv.shape)] + [anywhere] * len(pieces),
            row_block(heads_width),
            rows_of(heads_width),
            [pltpu.VMEM((2 * wide, qkv_width), bf16), piece_copies(pieces)],
            15,
            "attention",
        )(proc, lengths, second, rows_own, rows_other, prefix_kv, *pieces)

    def small_operands(w_xproj, conv_state, conv_bias, dt_bias, skip_gain, prefix_len, group_size):
        mix_weight = jnp.concatenate(
            [
                jnp.pad(w_xproj[:, :rank], ((0, 0), (0, 128 - rank))),
                jnp.pad(w_xproj[:, rank:], ((0, 0), (0, mixes - 128 - 2 * states))),
            ],
            axis=1,
        )
        return (
            mix_weight,
            conv_state,
            conv_bias[None],
            dt_bias[None],
            skip_gain[None],
            lax.dynamic_slice_in_dim(prefix_len, first_group, groups, 0),
            lax.dynamic_slice_in_dim(group_size, first_group, groups, 0),
        )

    plain = (w_xproj, conv_state, conv_bias, dt_bias, skip_gain, prefix_len, group_size)

    def convolve(rows_own, rows_other, pieces, small):
        return call(
            functools.partial(conv_kernel, slots, group_rows, len(pieces), half, 0),
            2,
            rows // tile,
            [
                row_block(wide),
                row_block(wide),
                whole(*conv_state.shape),
                whole(*conv_weight.shape),
                whole(1, channels),
                whole(channels, mixes),
            ]
            + [anywhere] * len(pieces),
            [row_block(channels), row_block(mixes)],
            [rows_of(channels), rows_of(mixes)],
            [pltpu.VMEM((2 * wide, channels), bf16), piece_copies(pieces)],
            14,
            "convolve",
        )(
            proc,
            second,
            rows_own,
            rows_other,
            small[1],
            conv_weight,
            small[2],
            small[0],
            *pieces,
        )

    def scan(first, count, conv_out, mix_own, mix_other, small, earlier=()):
        across = -(-channels // 128) * 128
        blocks = functools.partial(row_block, size=group_rows, first=first)
        return call(
            functools.partial(scan_kernel, slots),
            1,
            count,
            [
                blocks(channels),
                blocks(mixes),
                blocks(mixes),
                whole(rank, channels),
                whole(1, channels),
                whole(states, channels),
                whole(1, channels),
                group_block(*ssm_state.shape[1:], first=first),
            ]
            + [anywhere] * len(earlier),
            blocks(channels),
            rows_of(channels, f32),
            [pltpu.VMEM((group_rows, across), f32)] * 3
            + [pltpu.VMEM((states, across), f32)] * 2
            + [pltpu.VMEM((states, group_rows, 128), bf16)] * 2,
            4 * count,
            "scan_states",
            {9: 0} if earlier else None,
        )(
            proc,
            conv_out,
            mix_own,
            mix_other,
            dt_weight,
            small[3],
            decay_log,
            small[4],
            ssm_state,
            *earlier,
        )

    def gate(rows_own, rows_other, scanned, pieces):
        return call(
            functools.partial(gate_kernel, len(pieces), half, 0),
            1,
            rows // tile,
            [row_block(wide)] * 2 + [row_block(channels)] + [anywhere] * len(pieces),
            row_block(channels),
            rows_of(channels),
            [pltpu.VMEM((2 * wide, channels), bf16), piece_copies(pieces)],
            13,
            "gate",
        )(second, rows_own, rows_other, scanned, *pieces)

    def attn_out(heads, pieces):
        blocks = []
        for number in range(sections):
            if by_links:
                blocks += [
                    ((plane * row_axis + slot) * pad, pad)
                    for slot in (2 * number, 2 * number + 1)
                    for plane in range(2)
                ]
            else:
                blocks.append((0, half))
            if section_wide > section:
                blocks.append((None, section_wide - section))
        return call(
            functools.partial(attn_out_kernel, len(pieces), half, qkv_width, tuple(blocks)),
            1,
            rows // tile,
            [row_block(heads_width)] + [anywhere] * len(pieces),
            [row_block(columns)] * 2,
            [rows_of(columns)] * 2,
            [
                pltpu.VMEM((2 * wide, heads_width), bf16),
                pltpu.VMEM((2 * columns, heads_width), bf16),
                piece_copies(pieces),
            ],
            6,
            "attn_out",
        )(second, heads, *pieces)

    def ssm_out(gated, choices, pieces, ready=()):
        scalars = jnp.stack([second[0], inner.astype(i32) if by_links else second[0]])
        sums = 1 if ready else 0
        return call(
            functools.partial(ssm_out_kernel, choices, section // len(choices), len(ready)),
            1,
            rows // tile,
            [row_block(channels)]
            + [row_block(value.shape[1]) for value in ready]
            + [anywhere] * len(pieces),
            [row_block(section_wide)] * 2 + [row_block(2)] * sums,
            [rows_of(section_wide)] * 2 + [rows_of(2, f32)] * sums,
            [
                pltpu.VMEM((2 * section_wide, channels), bf16),
                pltpu.SemaphoreType.DMA((len(choices), 2)),
            ],
            8,
            "ssm_out",
        )(scalars, gated, *ready, *pieces)

    def squares(attn, ssm, earlier=None):
        if earlier is not None:
            operands, specs = [earlier], [row_block(2)]
        else:
            operands, specs = list(attn), [row_block(columns)] * 2
        return call(
            square_kernel,
            0,
            rows // tile,
            specs + [row_block(section_wide)] * 2,
            row_block(2),
            rows_of(2, f32),
            [],
            2,
            "squares",
        )(*operands, *ssm)

    def mix(part, x_keep, attn, ssm, own_squares, other_squares, gains, features_back, sizes):
        here = groups // pairs
        size = 2 * group_rows
        block = functools.partial(row_block, size=size, first=part * here // 2)
        return call(
            functools.partial(mixed_kernel, slots, part * here, sections, here),
            2,
            here // 2,
            [block(columns)] * 3
            + [block(section_wide)] * (2 * sections)
            + [block(2)] * 2
            + [whole(2, columns), whole(columns, width)],
            [anywhere] * here,
            [rows_of(width, count=group_rows)] * here,
            [pltpu.VMEM((here, group_rows, width), bf16), pltpu.SemaphoreType.DMA((here,))],
            4,
            "mixed_rows",
        )(
            proc,
            sizes,
            x_keep,
            *attn,
            *ssm,
            own_squares,
            other_squares,
            gains,
            features_back,
        )

    if by_links:

        def line_first(value):
            return along_z(value, Z_OUTER), along_z(value, Z_INNER)

        def line_second(first):
            near, middle = first
            return along_z(near, Z_INNER), along_z(middle, Z_ENDS), along_z(near, Z_FAR)

        inner = (row == 1) | (row == 2)

        def line_block(value, first, last):
            near, middle = first
            crossed, ends, far = last
            return jnp.concatenate(
                [value, near, jnp.where(inner, middle, ends), jnp.where(inner, crossed, far)],
                axis=0,
            )

        def plane_first(value):
            return swap_x(value), swap_y(value)

        def plane_second(first):
            by_x, by_y = first
            cut = by_x.shape[0] // 16 * 8
            return swap_y(by_x[:cut]), swap_x(by_y[cut:])

        ssm_p1 = plane_first(ssm_shard)
        conv_z1 = line_first(conv_shard)

        ssm_p1, conv_z1, tokens_late, serve_late, rep_late, row_late = tie(
            ssm_p1, conv_z1, tokens, serve_replica, rep, row
        )
        ssm_p2 = plane_second(ssm_p1)
        conv_z2 = line_second(conv_z1)
        proc = group_order(serve_late)
        rows_own = spread(inverse_rms(tokens_late), rep_late, row_late)

        conv_block = line_block(conv_shard, conv_z1, conv_z2)
        conv_block, ssm_p2, gate_shard, rows_own = tie(conv_block, ssm_p2, gate_shard, rows_own)
        conv_p1 = plane_first(conv_block)
        gate_z1 = line_first(gate_shard)
        gate_z1, plain = tie(gate_z1, plain)
        gate_z2 = line_second(gate_z1)
        small = small_operands(*plain)

        ssm_block = jnp.concatenate((ssm_shard,) + tuple(ssm_p1) + tuple(ssm_p2), axis=0)
        gate_block = line_block(gate_shard, gate_z1, gate_z2)
        conv_p1, gate_block, ssm_block, rows_own, rep_late, row_late, small = tie(
            conv_p1, gate_block, ssm_block, rows_own, rep, row, small
        )
        conv_p2 = plane_second(conv_p1)
        ssm_near, ssm_middle = line_first(ssm_block)
        rows_other = other_core(rows_own)
        keep_pick, gains, features_back = column_picks(rep_late, row_late)
        x_keep = place(keep_pick)

        conv_p2, gate_block, rows_other, attn_shard, x_keep, gains, features_back = tie(
            conv_p2, gate_block, rows_other, attn_shard, x_keep, gains, features_back
        )
        gate_p1 = plane_first(gate_block)
        conv_out, mix_own = convolve(
            rows_own, rows_other, (conv_block,) + tuple(conv_p1) + tuple(conv_p2), small
        )
        conv_out, mix_own, ssm_near, ssm_middle, attn_shard = tie(
            conv_out, mix_own, ssm_near, ssm_middle, attn_shard
        )
        mix_other = other_core(mix_own)
        attn_z1 = line_first(attn_shard)
        count = groups // 2
        scanned = scan(0, count, conv_out, mix_own, mix_other, small)

        gate_p1, attn_z1, scanned = tie(gate_p1, attn_z1, scanned)
        gate_p2 = plane_second(gate_p1)
        attn_z2 = line_second(attn_z1)
        scanned = scan(
            count, groups - count, conv_out, mix_own, mix_other, small, (scanned,)
        )
        attn_block = line_block(attn_shard, attn_z1, attn_z2)

        gate_p2, attn_block, ssm_near, ssm_middle, scanned = tie(
            gate_p2, attn_block, ssm_near, ssm_middle, scanned
        )
        attn_p1 = plane_first(attn_block)
        crossed = along_z(ssm_near, Z_INNER)
        ends = along_z(ssm_middle, Z_ENDS)
        gated = gate(rows_own, rows_other, scanned, (gate_block,) + tuple(gate_p1) + tuple(gate_p2))

        attn_p1, gated = tie(attn_p1, gated)
        attn_p2 = plane_second(attn_p1)
        keep_early, send_early = ssm_out(gated, (1, 1), (ssm_block, ssm_near))
        crossed, ends, ssm_near, keep_early, attn_p2, attn_block = tie(
            crossed, ends, ssm_near, keep_early, attn_p2, attn_block
        )
        far = along_z(ssm_near, Z_FAR)
        got_early = other_core(send_early)
        attn_pieces = (attn_block,) + tuple(attn_p1) + tuple(attn_p2)
        heads = attention(rows_own, rows_other, attn_pieces, small[5])
        keep_attn, send_attn = attn_out(heads, attn_pieces)
        send_attn, far = tie(send_attn, far)
        got_attn = other_core(send_attn)
        attn = [keep_attn, got_attn]

        late_pieces = (ssm_middle, ends, crossed, far)
        keep_late, send_late, sums = ssm_out(
            gated, (2, 2), late_pieces, attn + [keep_early, got_early]
        )
        got_late = other_core(send_late)
        sums = squares(attn, [keep_late, got_late], sums)
        other_sums = other_core(sums)
        ssm = [keep_early, got_early, keep_late, got_late]
        received = []
        for part in range(pairs):
            mixed = mix(part, x_keep, attn, ssm, sums, other_sums, gains, features_back, small[6])
            received.append(
                (
                    mixed[0],
                    swap_x(mixed[1]),
                    swap_y(mixed[2]),
                    lax.ppermute(mixed[3], "rep", D_PAIRS),
                )
            )
        by_source = [jnp.stack([part[index] for part in received]) for index in range(rep_count)]
        for bit in (1, 2):
            swapped = (rep & bit) != 0
            by_source = [
                jnp.where(swapped, by_source[index ^ bit], by_source[index])
                for index in range(rep_count)
            ]
        mixed = jnp.concatenate(by_source, axis=0)
    else:

        def gathered(value):
            return lax.all_gather(value, ("rep", "tr"), axis=0, tiled=True)

        proc = group_order(serve_replica)
        small = small_operands(*plain)
        rows_own = spread(inverse_rms(tokens), rep, row)
        rows_other = other_core(rows_own)
        keep_pick, gains, features_back = column_picks(rep, row)
        x_keep = place(keep_pick)
        attn_pieces = (gathered(attn_shard),)
        heads = attention(rows_own, rows_other, attn_pieces, small[5])
        conv_out, mix_own = convolve(rows_own, rows_other, (gathered(conv_shard),), small)
        scanned = scan(0, groups, conv_out, mix_own, other_core(mix_own), small)
        gated = gate(rows_own, rows_other, scanned, (gathered(gate_shard),))
        keep_attn, send_attn = attn_out(heads, attn_pieces)
        attn = [keep_attn, other_core(send_attn)]
        kept, sent = ssm_out(gated, (1,), (gathered(ssm_shard),))
        ssm = [kept, other_core(sent)]
        sums = squares(attn, ssm)
        other_sums = other_core(sums)
        received = [
            jnp.stack(
                mix(part, x_keep, attn, ssm, sums, other_sums, gains, features_back, small[6])
            )
            for part in range(pairs)
        ]
        mixed = jnp.stack(received, axis=1).reshape(groups, group_rows, width)
        mixed = lax.all_to_all(mixed, "rep", split_axis=0, concat_axis=0, tiled=True)
    return mixed.reshape(groups, slots, steps, width)


def solution(mesh):
    placed = (
        P(("rep", "tr"), None, None, "tc"),
        P(("rep", "tr"), None, "tc"),
        P(("rep", "tr"), None, "tc"),
        P(("rep", "tr"), None, "tc"),
        P(),
        P(),
        P(),
        P("tc"),
        P(("rep", "tr"), "tc"),
        P(("rep", "tr"), "tc"),
        P(("rep", "tr"), None, "tc"),
        P(None, "tc"),
        P("tc"),
        P("tc", None),
        P(None, "tc"),
        P("tc"),
        P(None, "tc"),
        P("tc"),
        P("tc", ("rep", "tr")),
        P("tc", ("rep", "tr")),
        P(),
        P(),
    )
    return jax.shard_map(
        local,
        mesh=mesh,
        in_specs=placed,
        out_specs=P(("rep", "tr"), None, None, "tc"),
        check_vma=False,
    )
```

```python
import functools

import jax
import jax.numpy as jnp
from jax import lax
from jax.experimental import pallas as pl
from jax.experimental.pallas import tpu as pltpu
from jax.sharding import PartitionSpec as P

D = 1600
HD = 64
QH = 16
KVH = 4

EPSILON = 1e-06
LOG2_E = 1.4426950408889634

X_PAIRS = ((0, 1), (1, 0), (2, 3), (3, 2))
Y_PAIRS = ((0, 2), (2, 0), (1, 3), (3, 1))
D_PAIRS = ((0, 3), (3, 0), (1, 2), (2, 1))
Z_OUTER = ((0, 1), (1, 0), (2, 3), (3, 2))
Z_INNER = ((1, 2), (2, 1))
Z_ENDS = ((1, 0), (2, 3))
Z_FAR = ((2, 0), (1, 3))
Z_SLOTS = ((0, 1, 2, 3), (1, 0, 2, 3), (2, 3, 1, 0), (3, 2, 1, 0))

VMEM_LIMIT = 56 * 1024 * 1024


def params():
    return pltpu.CompilerParams(vmem_limit_bytes=VMEM_LIMIT)


def cost(flops, size):
    return pl.CostEstimate(flops=int(flops), bytes_accessed=int(size), transcendentals=0)


def tie(*values):
    return lax.optimization_barrier(values)


def swap_x(value):
    return lax.ppermute(value, "rep", X_PAIRS)


def swap_y(value):
    return lax.ppermute(value, "rep", Y_PAIRS)


def along_z(value, pairs):
    return lax.ppermute(value, "tr", pairs)


def other_core(value):
    return lax.ppermute(value, "tc", ((0, 1), (1, 0)))


def load_halves(pieces, target, sems, second, half, wide, column=0):
    width = target.shape[1]
    if wide > half:
        gap = jnp.zeros((wide - half, width), target.dtype)
        target[half:wide, :] = gap
        target[wide + half :, :] = gap
    copies = []
    start = 0
    for piece in pieces:
        count = piece.shape[0]
        for low in range(0, count, half):
            size = min(half, count)
            at_first = start < half
            place = (second if at_first else 1 - second) * wide + start % half
            copies.append(
                pltpu.make_async_copy(
                    piece.at[pl.ds(low, size), pl.ds(column, width)],
                    target.at[pl.ds(pl.multiple_of(place, 16), size), :],
                    sems.at[len(copies)],
                )
            )
            start += size
    for copy in copies:
        copy.start()
    for copy in copies:
        copy.wait()


def silu(value):
    scaled = 0.5 * value
    return scaled + scaled * jnp.tanh(scaled)


def row_mover(slots, steps, inward):
    count = slots * steps
    to_row = lax.broadcasted_iota(jnp.int32, (count, count), 0)
    from_row = lax.broadcasted_iota(jnp.int32, (count, count), 1)
    if inward:
        source = (to_row % slots) * steps + to_row // slots
    else:
        source = (to_row % steps) * slots + to_row // steps
    return jnp.where(from_row == source, 1.0, 0.0).astype(jnp.bfloat16)


def both_halves(rows_own, rows_other, weight):
    rows = jnp.concatenate([rows_own[...], rows_other[...]], axis=1)
    return jnp.dot(rows, weight[...], preferred_element_type=jnp.float32)


def exact_dot(left, right):
    return jnp.dot(left, right, preferred_element_type=jnp.float32).astype(jnp.bfloat16)


def spread_kernel(slots, proc, x, inv_rms, gain, pick, out):
    normed = (x[0].astype(jnp.float32) * inv_rms[0] * gain[...]).astype(jnp.bfloat16)
    mover = row_mover(slots, x.shape[1] // slots, True)
    out[...] = exact_dot(exact_dot(mover, normed), pick[...])


def place_kernel(slots, proc, x, pick, out):
    mover = row_mover(slots, x.shape[1] // slots, True)
    out[...] = exact_dot(exact_dot(mover, x[0]), pick[...])


def attention_kernel(
    slots,
    group_rows,
    kv_here,
    per_kv,
    count,
    half,
    first_column,
    proc,
    lengths,
    second,
    rows_own,
    rows_other,
    cache,
    *rest,
):
    pieces, (out, weight, sems) = rest[:count], rest[count:]
    tile = pl.program_id(0)

    @pl.when(tile == 0)
    def _():
        load_halves(pieces, weight, sems, second[0], half, weight.shape[0] // 2, first_column)

    made = both_halves(rows_own, rows_other, weight).astype(jnp.bfloat16)
    here = made.shape[0] // group_rows
    query_width = kv_here * per_kv * HD
    positions = cache.shape[1]
    stacked = per_kv * group_rows
    row_id = lax.broadcasted_iota(jnp.int32, (stacked, group_rows), 0) % group_rows
    column_id = lax.broadcasted_iota(jnp.int32, (stacked, group_rows), 1)
    own_mask = (row_id % slots == column_id % slots) & (column_id // slots <= row_id // slots)
    column = lax.broadcasted_iota(jnp.int32, (stacked, positions), 1)
    contract = (((1,), (1,)), ((), ()))
    scale = HD ** (-0.5)
    for index in range(here):
        group = proc[tile * here + index]
        prefix_mask = column < lengths[group]
        block = made[index * group_rows : (index + 1) * group_rows]
        past = cache[group]
        results = []
        for head in range(kv_here):
            query = jnp.concatenate(
                [
                    block[:, (head * per_kv + j) * HD : (head * per_kv + j + 1) * HD]
                    for j in range(per_kv)
                ],
                axis=0,
            )
            base = query_width + head * 2 * HD
            key_new = block[:, base : base + HD]
            value_new = block[:, base + HD : base + 2 * HD]
            key_old = past[:, head * 2 * HD : head * 2 * HD + HD]
            value_old = past[:, head * 2 * HD + HD : (head + 1) * 2 * HD]
            old = lax.dot_general(query, key_old, contract, preferred_element_type=jnp.float32)
            new = lax.dot_general(query, key_new, contract, preferred_element_type=jnp.float32)
            old = jnp.where(prefix_mask, old * scale, -jnp.inf)
            new = jnp.where(own_mask, new * scale, -jnp.inf)
            top = jnp.maximum(
                jnp.max(old, axis=1, keepdims=True), jnp.max(new, axis=1, keepdims=True)
            )
            old = jnp.exp(old - top)
            new = jnp.exp(new - top)
            total = jnp.sum(old, axis=1, keepdims=True) + jnp.sum(new, axis=1, keepdims=True)
            value = jnp.dot(
                old.astype(jnp.bfloat16), value_old, preferred_element_type=jnp.float32
            ) + jnp.dot(new.astype(jnp.bfloat16), value_new, preferred_element_type=jnp.float32)
            value = (value / total).astype(jnp.bfloat16)
            for j in range(per_kv):
                results.append(value[j * group_rows : (j + 1) * group_rows])
        out[index * group_rows : (index + 1) * group_rows, :] = jnp.concatenate(results, axis=1)


def conv_kernel(
    slots,
    group_rows,
    count,
    half,
    first_column,
    proc,
    second,
    rows_own,
    rows_other,
    history,
    taps,
    bias,
    mix_weight,
    *rest,
):
    pieces, (out, out_mix, weight, sems) = rest[:count], rest[count:]
    tile = pl.program_id(0)

    @pl.when(tile == 0)
    def _():
        load_halves(pieces, weight, sems, second[0], half, weight.shape[0] // 2, first_column)

    made = both_halves(rows_own, rows_other, weight)
    here = made.shape[0] // group_rows
    steps = group_rows // slots
    tap_count = taps.shape[0]
    past = history.shape[1]
    for index in range(here):
        start = index * group_rows
        state = history[proc[tile * here + index]]
        sequence = [
            jnp.broadcast_to(state[k : k + 1, :], (slots, made.shape[1])) for k in range(past)
        ] + [made[start + step * slots : start + (step + 1) * slots] for step in range(steps)]
        for step in range(steps):
            value = bias[...]
            for tap in range(tap_count):
                value = value + taps[tap : tap + 1, :] * sequence[step + tap]
            out[start + step * slots : start + (step + 1) * slots, :] = silu(value).astype(
                jnp.bfloat16
            )
    out_mix[...] = jnp.dot(
        out[...], mix_weight[...], preferred_element_type=jnp.float32
    ).astype(jnp.bfloat16)


def softplus(value):
    small = jnp.exp(-jnp.abs(value))
    series = small * (1.0 - small * (0.5 - small * (1.0 / 3.0)))
    return jnp.maximum(value, 0.0) + jnp.where(small < 0.01, series, jnp.log(1.0 + small))


def scan_kernel(
    slots, proc, conv, mix_own, mix_other, step_weight, step_bias, decay_log, skip, state, *rest
):
    out, *scratch = rest[-8:]
    step_scratch, drive_scratch, out_scratch, rate_scratch, state_scratch, in_mix, out_mix = scratch
    lanes = 128
    kind = jnp.bfloat16
    rank = step_weight.shape[0]
    states, channels = decay_log.shape
    total_rows = conv.shape[0]
    mix = mix_own[...].astype(jnp.float32) + mix_other[...].astype(jnp.float32)
    raw = (
        jnp.dot(mix[:, :rank].astype(kind), step_weight[...], preferred_element_type=jnp.float32)
        + step_bias[...]
    )
    step = softplus(raw)
    value = conv[...].astype(jnp.float32)
    step_scratch[:, :channels] = step
    drive_scratch[:, :channels] = step * value
    rate_scratch[:, :channels] = -jnp.exp(decay_log[...]) * LOG2_E
    state_scratch[:, :channels] = state[0]
    for n in range(states):
        in_mix[n] = jnp.broadcast_to(mix[:, 128 + n : 129 + n], (total_rows, lanes)).astype(kind)
        out_mix[n] = jnp.broadcast_to(
            mix[:, 128 + states + n : 129 + states + n], (total_rows, lanes)
        ).astype(kind)

    def one(chunk, carry):
        columns = pl.ds(pl.multiple_of(chunk * lanes, lanes), lanes)

        def spread(source, n):
            return jnp.broadcast_to(source[n : n + 1, columns], (slots, lanes)).astype(kind)

        held = [spread(state_scratch, n) for n in range(states)]
        for start in range(0, total_rows, slots):
            here = pl.ds(start, slots)
            size = step_scratch[here, columns].astype(kind)
            drive = drive_scratch[here, columns].astype(kind)
            total = None
            for first in range(0, states, 4):
                part = None
                for n in range(first, first + 4):
                    held[n] = (
                        jnp.exp2(size * spread(rate_scratch, n)) * held[n]
                        + drive * in_mix[n, here, :]
                    )
                    term = held[n] * out_mix[n, here, :]
                    part = term if part is None else part + term
                part = part.astype(jnp.float32)
                total = part if total is None else total + part
            out_scratch[here, columns] = total
        return carry

    lax.fori_loop(0, step_scratch.shape[1] // lanes, one, 0)
    out[...] = out_scratch[:, :channels] + skip[...] * value


def gate_kernel(count, half, first_column, second, rows_own, rows_other, scanned, *rest):
    pieces, (out, weight, sems) = rest[:count], rest[count:]

    @pl.when(pl.program_id(0) == 0)
    def _():
        load_halves(pieces, weight, sems, second[0], half, weight.shape[0] // 2, first_column)

    gate = both_halves(rows_own, rows_other, weight)
    out[...] = (scanned[...] * silu(gate)).astype(jnp.bfloat16)


def transposed_dot(left, right):
    return lax.dot_general(
        left, right, (((1,), (1,)), ((), ())), preferred_element_type=jnp.float32
    ).astype(jnp.bfloat16)


def attn_out_kernel(count, half, first_column, blocks, second, heads, *rest):
    pieces, (keep, send, raw, weight, sems) = rest[:count], rest[count:]
    wide = raw.shape[0] // 2
    columns = weight.shape[0] // 2

    @pl.when(pl.program_id(0) == 0)
    def _():
        load_halves(pieces, raw, sems, second[0], half, wide, first_column)
        loaded = raw[...].astype(jnp.float32)
        for index in range(2):
            parts = [
                jnp.zeros((size, loaded.shape[1]), jnp.float32)
                if at is None
                else loaded[index * wide + at : index * wide + at + size]
                for at, size in blocks
            ]
            weight[index * columns : (index + 1) * columns, :] = jnp.concatenate(
                parts, axis=0
            ).astype(weight.dtype)

    attended = heads[...]
    keep[...] = transposed_dot(attended, weight[:columns, :])
    send[...] = transposed_dot(attended, weight[columns:, :])


def ssm_out_kernel(slot_choices, part, scalars, gated, *rest):
    count = sum(slot_choices)
    pieces, (keep, send, weight, sems) = rest[:count], rest[count:]
    wide = weight.shape[0] // 2
    filled = part * len(slot_choices)
    second = scalars[0]

    @pl.when(pl.program_id(0) == 0)
    def _():
        if wide > filled:
            gap = jnp.zeros((wide - filled, weight.shape[1]), weight.dtype)
            weight[filled:wide, :] = gap
            weight[wide + filled :, :] = gap

        def copies(source, slot):
            for index, base in ((0, second), (1, 1 - second)):
                yield pltpu.make_async_copy(
                    source.at[pl.ds(pl.multiple_of(base * part, 16), part), :],
                    weight.at[pl.ds(index * wide + slot * part, part), :],
                    sems.at[slot, index],
                )

        at = 0
        firsts = []
        for slot, choices in enumerate(slot_choices):
            firsts.append(pieces[at])
            if choices == 1:
                for copy in copies(pieces[at], slot):
                    copy.start()
            else:
                for choice in range(2):

                    @pl.when(scalars[1] == 1 - choice)
                    def _(piece=pieces[at + choice], slot=slot):
                        for copy in copies(piece, slot):
                            copy.start()

            at += choices
        for slot, piece in enumerate(firsts):
            for copy in copies(piece, slot):
                copy.wait()

    value = gated[...]
    send[...] = transposed_dot(value, weight[wide:, :])
    keep[...] = transposed_dot(value, weight[:wide, :])


def square_sum(keep, got):
    value = keep[...].astype(jnp.float32) + got[...].astype(jnp.float32)
    return jnp.sum(value * value, axis=1, keepdims=True)


def square_kernel(*refs):
    *refs, out = refs
    out[:, 0:1] = square_sum(refs[0], refs[1])
    total = square_sum(refs[2], refs[3])
    for index in range(4, len(refs), 2):
        total += square_sum(refs[index], refs[index + 1])
    out[:, 1:2] = total


def mixed_kernel(slots, first, sections, here, proc, sizes, x_keep, keep_attn, got_attn, *rest):
    ssm_refs = rest[: 2 * sections]
    own_squares, other_squares, gains, features = rest[2 * sections : 2 * sections + 4]
    outs = rest[2 * sections + 4 : 2 * sections + 4 + here]
    made, sems = rest[2 * sections + 4 + here :]
    step = pl.program_id(0)
    ssm = jnp.concatenate(
        [
            keep[...].astype(jnp.float32) + got[...].astype(jnp.float32)
            for keep, got in zip(ssm_refs[::2], ssm_refs[1::2])
        ],
        axis=1,
    )
    attn = keep_attn[...].astype(jnp.float32) + got_attn[...].astype(jnp.float32)
    scales = lax.rsqrt((own_squares[...] + other_squares[...]) / D + EPSILON)
    branch = 0.5 * (
        gains[0:1, :] * attn * scales[:, 0:1] + gains[1:2, :] * ssm * scales[:, 1:2]
    )
    mixed = (x_keep[...].astype(jnp.float32) + branch).astype(jnp.bfloat16)
    placed = exact_dot(mixed, features[...])
    size = made.shape[1]
    in_step = mixed.shape[0] // size
    outward = row_mover(slots, size // slots, False)
    slot = lax.broadcasted_iota(jnp.int32, (size, 1), 0) // (size // slots)

    def copy(number):
        return pltpu.make_async_copy(made.at[number], outs[number], sems.at[number])

    for index in range(in_step):
        number = step * in_step + index
        rows = exact_dot(outward, placed[index * size : (index + 1) * size])
        live = slot < sizes[proc[first + number]]
        made[number] = jnp.where(live, rows, jnp.zeros_like(rows))
    for number in range(here):

        @pl.when(step == number // in_step)
        def _(number=number):
            copy(number).start()

    @pl.when(step == here // in_step - 1)
    def _():
        for number in range(here):
            copy(number).wait()


def local(
    tokens,
    prefix_kv,
    ssm_state,
    conv_state,
    prefix_len,
    group_size,
    serve_replica,
    in_gain,
    w_query,
    w_keyval,
    w_inner,
    conv_weight,
    conv_bias,
    w_xproj,
    dt_weight,
    dt_bias,
    decay_log,
    skip_gain,
    w_attn_out,
    w_ssm_out,
    attn_gain,
    ssm_gain,
):
    rep_count = lax.axis_size("rep")
    row_axis = lax.axis_size("tr")
    tensor_count = lax.axis_size("tc")
    rep = lax.axis_index("rep")
    row = lax.axis_index("tr")
    core = lax.axis_index("tc")
    groups, slots, steps, width = tokens.shape
    pairs = groups // rep_count
    kv_here = KVH // tensor_count
    per_kv = QH // KVH
    heads_width = QH // tensor_count * HD
    group_rows = slots * steps
    rows = groups * group_rows
    tile = groups // 4 * group_rows
    channels = w_inner.shape[2]
    shards = rep_count * row_axis
    shard = w_query.shape[0]
    pad = -(-shard // 8) * 8
    depth = shards * pad
    half = depth // 2
    wide = -(-half // 128) * 128
    by_links = rep_count == 4 and row_axis == 4
    sections = 2 if by_links else 1
    section = half // sections
    section_wide = -(-section // 128) * 128
    columns = sections * section_wide
    bf16 = jnp.bfloat16
    f32 = jnp.float32
    i32 = jnp.int32

    def padded(value):
        return jnp.pad(value, ((0, pad - shard), (0, 0)))

    ssm_shard = padded(w_ssm_out.T)
    conv_shard = padded(w_inner[:, 0])
    def shard_behind(w_query, w_keyval, w_attn_out, w_gate):
        return padded(jnp.concatenate([w_query, w_keyval, w_attn_out.T, w_gate], axis=1))

    qkv_width = w_query.shape[1] + w_keyval.shape[1]
    attn_width = qkv_width + heads_width
    rank, states = dt_weight.shape[0], decay_log.shape[0]
    mixes = 256

    def feature_at(column, lines_outside, rep, row):
        inside = column < half
        if lines_outside:
            inside = column % section_wide < section
            column = column // section_wide * section + column % section_wide
        block, offset = column // pad, column % pad
        if by_links:
            if lines_outside:
                slot, plane = block // 2, block % 2
            else:
                slot, plane = block % row_axis, block // row_axis
            low = row < 2
            line = jnp.where(
                slot == 0,
                row,
                jnp.where(
                    slot == 1,
                    row ^ 1,
                    jnp.where(slot == 2, jnp.where(low, 2, 1), jnp.where(low, 3, 0)),
                ),
            )
            block = ((rep % 2) ^ plane) * row_axis + line
        return jnp.where((offset < shard) & inside, block * shard + offset, -1)

    def picker(shape, column_dim, lines_outside, rep, row):
        line = tuple(size if dim == column_dim else 1 for dim, size in enumerate(shape))
        column = lax.broadcasted_iota(i32, line, column_dim)
        (source,) = tie(feature_at(column, lines_outside, rep, row))
        return lax.broadcasted_iota(i32, shape, 1 - column_dim) == source

    def column_picks(rep, row):
        keep_pick = picker((width, columns), 1, True, rep, row)
        gains = jnp.stack([attn_gain, ssm_gain])
        gains = lax.dynamic_slice_in_dim(gains, core * width, width, 1)
        gains = jnp.sum(jnp.where(keep_pick[None], gains[:, :, None], 0.0), axis=1)
        features_back = picker((columns, width), 0, True, rep, row).astype(bf16)
        return keep_pick.astype(bf16), gains, features_back

    second = ((rep // 2) ^ core if by_links else core).astype(i32)[None]

    def group_order(serve_replica):
        served = lax.dynamic_slice_in_dim(serve_replica, first_group, groups, 0)
        target = served ^ rep if by_links else served
        ids = jnp.arange(groups, dtype=i32)
        same = (served[:, None] == served[None, :]) & (ids[None, :] < ids[:, None])
        places = jnp.sum(same.astype(i32), axis=1) * rep_count + target
        return jnp.sum(
            jnp.where(places[None, :] == ids[:, None], ids[None, :], 0), axis=1
        ).astype(i32)

    def inverse_rms(tokens):
        wide_rows = tokens.reshape(groups, group_rows, width).astype(f32)
        square_sums = lax.psum(jnp.sum(wide_rows * wide_rows, axis=2), "tc")
        return lax.rsqrt(square_sums / D + EPSILON)[:, :, None]

    first_group = (rep * row_axis + row) * groups
    def row_block(columns, size=tile, first=0):
        return pl.BlockSpec((size, columns), lambda g, *_: (g + first, 0))

    def whole(*shape):
        return pl.BlockSpec(shape, lambda g, *_: (0,) * len(shape))

    def group_block(*shape, first=0):
        return pl.BlockSpec(
            (1,) + shape, lambda g, proc, *_: (proc[g + first],) + (0,) * len(shape)
        )

    anywhere = pl.BlockSpec(memory_space=pl.ANY)

    def rows_of(columns, kind=bf16, count=rows):
        return jax.ShapeDtypeStruct((count, columns), kind)

    def call(kernel, scalars, grid, in_specs, out_specs, out_shape, scratch, spend, name, alias=None):
        return pl.pallas_call(
            kernel,
            grid_spec=pltpu.PrefetchScalarGridSpec(
                num_scalar_prefetch=scalars,
                grid=(grid,),
                in_specs=in_specs,
                out_specs=out_specs,
                scratch_shapes=scratch,
            ),
            out_shape=out_shape,
            input_output_aliases=alias or {},
            compiler_params=params(),
            cost_estimate=cost(spend * 1.0e7, rows * 4),
            name=name,
        )

    def piece_copies(pieces):
        return pltpu.SemaphoreType.DMA((max(len(pieces), 2),))

    def spread(inv, rep, row):
        spread_pick = picker((width, wide), 1, False, rep, row).astype(bf16)
        return call(
            functools.partial(spread_kernel, slots),
            1,
            groups,
            [
                group_block(group_rows, width),
                group_block(group_rows, 1),
                whole(1, width),
                whole(width, wide),
            ],
            row_block(wide, group_rows),
            rows_of(wide),
            [],
            8,
            "spread_rows",
        )(proc, tokens.reshape(groups, group_rows, width), inv, in_gain[None], spread_pick)

    def place(keep_pick):
        return call(
            functools.partial(place_kernel, slots),
            1,
            groups,
            [group_block(group_rows, width), whole(width, columns)],
            row_block(columns, group_rows),
            rows_of(columns),
            [],
            8,
            "place_rows",
        )(proc, tokens.reshape(groups, group_rows, width), keep_pick)

    def attention(rows_own, rows_other, pieces, lengths):
        return call(
            functools.partial(
                attention_kernel, slots, group_rows, kv_here, per_kv, len(pieces), half, 0
            ),
            3,
            rows // tile,
            [row_block(wide)] * 2 + [whole(*prefix_kv.shape)] + [anywhere] * len(pieces),
            row_block(heads_width),
            rows_of(heads_width),
            [pltpu.VMEM((2 * wide, qkv_width), bf16), piece_copies(pieces)],
            15,
            "attention",
        )(proc, lengths, second, rows_own, rows_other, prefix_kv, *pieces)

    def small_operands(w_xproj, conv_state, conv_bias, dt_bias, skip_gain, prefix_len, group_size):
        mix_weight = jnp.concatenate(
            [
                jnp.pad(w_xproj[:, :rank], ((0, 0), (0, 128 - rank))),
                jnp.pad(w_xproj[:, rank:], ((0, 0), (0, mixes - 128 - 2 * states))),
            ],
            axis=1,
        )
        return (
            mix_weight,
            conv_state,
            conv_bias[None],
            dt_bias[None],
            skip_gain[None],
            lax.dynamic_slice_in_dim(prefix_len, first_group, groups, 0),
            lax.dynamic_slice_in_dim(group_size, first_group, groups, 0),
        )

    plain = (w_xproj, conv_state, conv_bias, dt_bias, skip_gain, prefix_len, group_size)

    def convolve(rows_own, rows_other, pieces, small):
        return call(
            functools.partial(conv_kernel, slots, group_rows, len(pieces), half, 0),
            2,
            rows // tile,
            [
                row_block(wide),
                row_block(wide),
                whole(*conv_state.shape),
                whole(*conv_weight.shape),
                whole(1, channels),
                whole(channels, mixes),
            ]
            + [anywhere] * len(pieces),
            [row_block(channels), row_block(mixes)],
            [rows_of(channels), rows_of(mixes)],
            [pltpu.VMEM((2 * wide, channels), bf16), piece_copies(pieces)],
            14,
            "convolve",
        )(
            proc,
            second,
            rows_own,
            rows_other,
            small[1],
            conv_weight,
            small[2],
            small[0],
            *pieces,
        )

    def scan(first, count, conv_out, mix_own, mix_other, small, earlier=()):
        across = -(-channels // 128) * 128
        blocks = functools.partial(row_block, size=group_rows, first=first)
        return call(
            functools.partial(scan_kernel, slots),
            1,
            count,
            [
                blocks(channels),
                blocks(mixes),
                blocks(mixes),
                whole(rank, channels),
                whole(1, channels),
                whole(states, channels),
                whole(1, channels),
                group_block(*ssm_state.shape[1:], first=first),
            ]
            + [anywhere] * len(earlier),
            blocks(channels),
            rows_of(channels, f32),
            [pltpu.VMEM((group_rows, across), f32)] * 3
            + [pltpu.VMEM((states, across), f32)] * 2
            + [pltpu.VMEM((states, group_rows, 128), bf16)] * 2,
            4 * count,
            "scan_states",
            {9: 0} if earlier else None,
        )(
            proc,
            conv_out,
            mix_own,
            mix_other,
            dt_weight,
            small[3],
            decay_log,
            small[4],
            ssm_state,
            *earlier,
        )

    def gate(rows_own, rows_other, scanned, pieces, first_column):
        return call(
            functools.partial(gate_kernel, len(pieces), half, first_column),
            1,
            rows // tile,
            [row_block(wide)] * 2 + [row_block(channels)] + [anywhere] * len(pieces),
            row_block(channels),
            rows_of(channels),
            [pltpu.VMEM((2 * wide, channels), bf16), piece_copies(pieces)],
            13,
            "gate",
        )(second, rows_own, rows_other, scanned, *pieces)

    def attn_out(heads, pieces):
        blocks = []
        for number in range(sections):
            if by_links:
                blocks += [
                    ((plane * row_axis + slot) * pad, pad)
                    for slot in (2 * number, 2 * number + 1)
                    for plane in range(2)
                ]
            else:
                blocks.append((0, half))
            if section_wide > section:
                blocks.append((None, section_wide - section))
        return call(
            functools.partial(attn_out_kernel, len(pieces), half, qkv_width, tuple(blocks)),
            1,
            rows // tile,
            [row_block(heads_width)] + [anywhere] * len(pieces),
            [row_block(columns)] * 2,
            [rows_of(columns)] * 2,
            [
                pltpu.VMEM((2 * wide, heads_width), bf16),
                pltpu.VMEM((2 * columns, heads_width), bf16),
                piece_copies(pieces),
            ],
            6,
            "attn_out",
        )(second, heads, *pieces)

    def ssm_out(gated, choices, pieces):
        scalars = jnp.stack([second[0], inner.astype(i32) if by_links else second[0]])
        return call(
            functools.partial(ssm_out_kernel, choices, section // len(choices)),
            1,
            rows // tile,
            [row_block(channels)] + [anywhere] * len(pieces),
            [row_block(section_wide)] * 2,
            [rows_of(section_wide)] * 2,
            [
                pltpu.VMEM((2 * section_wide, channels), bf16),
                pltpu.SemaphoreType.DMA((len(choices), 2)),
            ],
            8,
            "ssm_out",
        )(scalars, gated, *pieces)

    def squares(attn, ssm):
        return call(
            square_kernel,
            0,
            rows // tile,
            [row_block(columns)] * 2 + [row_block(section_wide)] * len(ssm),
            row_block(2),
            rows_of(2, f32),
            [],
            2,
            "squares",
        )(*attn, *ssm)

    def mix(part, x_keep, attn, ssm, own_squares, other_squares, gains, features_back, sizes):
        here = groups // pairs
        size = 2 * group_rows
        block = functools.partial(row_block, size=size, first=part * here // 2)
        return call(
            functools.partial(mixed_kernel, slots, part * here, sections, here),
            2,
            here // 2,
            [block(columns)] * 3
            + [block(section_wide)] * (2 * sections)
            + [block(2)] * 2
            + [whole(2, columns), whole(columns, width)],
            [anywhere] * here,
            [rows_of(width, count=group_rows)] * here,
            [pltpu.VMEM((here, group_rows, width), bf16), pltpu.SemaphoreType.DMA((here,))],
            4,
            "mixed_rows",
        )(
            proc,
            sizes,
            x_keep,
            *attn,
            *ssm,
            own_squares,
            other_squares,
            gains,
            features_back,
        )

    if by_links:

        def line_first(value):
            return along_z(value, Z_OUTER), along_z(value, Z_INNER)

        def line_second(first):
            near, middle = first
            return along_z(near, Z_INNER), along_z(middle, Z_ENDS), along_z(near, Z_FAR)

        inner = (row == 1) | (row == 2)

        def line_block(value, first, last):
            near, middle = first
            crossed, ends, far = last
            return jnp.concatenate(
                [value, near, jnp.where(inner, middle, ends), jnp.where(inner, crossed, far)],
                axis=0,
            )

        def plane_first(value):
            return swap_x(value), swap_y(value)

        def plane_second(first):
            by_x, by_y = first
            cut = by_x.shape[0] // 16 * 8
            return swap_y(by_x[:cut]), swap_x(by_y[cut:])

        def upper(value, first):
            return jnp.concatenate([value, first[0]], axis=0)

        def lower(first, last):
            crossed, ends, far = last
            return jnp.concatenate(
                [jnp.where(inner, first[1], ends), jnp.where(inner, crossed, far)], axis=0
            )

        def left(values):
            return tuple(value[:, :attn_width] for value in values)

        def right(values):
            return tuple(value[:, attn_width:] for value in values)

        ssm_plane = plane_first(ssm_shard) + (lax.ppermute(ssm_shard, "rep", D_PAIRS),)
        conv_z1 = line_first(conv_shard)
        inv_rms = inverse_rms(tokens)

        ssm_x, ssm_y, ssm_corner = ssm_plane
        (
            conv_z1,
            conv_shard,
            ssm_x,
            ssm_y,
            inv_rms,
            serve_late,
            rep_late,
            row_late,
            late_weights,
        ) = tie(
            conv_z1,
            conv_shard,
            ssm_x,
            ssm_y,
            inv_rms,
            serve_replica,
            rep,
            row,
            (w_query, w_keyval, w_attn_out, w_inner[:, 1]),
        )
        conv_z2 = line_second(conv_z1)
        conv_top_own = upper(conv_shard, conv_z1)
        conv_top = plane_first(conv_top_own)
        proc = group_order(serve_late)
        rows_own = spread(inv_rms, rep_late, row_late)
        back_shard = shard_behind(*late_weights)

        conv_bottom_own = lower(conv_z1, conv_z2)
        conv_top, conv_bottom_own, back_shard, rows_own, plain, rep_late, row_late, ssm_corner = tie(
            conv_top, conv_bottom_own, back_shard, rows_own, plain, rep, row, ssm_corner
        )
        ssm_plane = (ssm_x, ssm_y, ssm_corner)
        conv_bottom = plane_first(conv_bottom_own)
        back_z1 = line_first(back_shard)
        rows_other = other_core(rows_own)
        small = small_operands(*plain)
        picks = column_picks(rep_late, row_late)

        conv_top, conv_bottom, back_z1, small, rows_other, ssm_plane, picks = tie(
            conv_top, conv_bottom, back_z1, small, rows_other, ssm_plane, picks
        )
        keep_pick, gains, features_back = picks
        conv_corner = (swap_y(conv_top[0]), swap_x(conv_bottom[1]))
        back_z2 = line_second(back_z1)
        ssm_block = jnp.concatenate((ssm_shard,) + ssm_plane, axis=0)
        x_keep = place(keep_pick)

        conv_corner, ssm_block, x_keep, gains, features_back = tie(
            conv_corner, ssm_block, x_keep, gains, features_back
        )
        conv_out, mix_own = convolve(
            rows_own,
            rows_other,
            (conv_top_own, conv_bottom_own, conv_top[0], conv_bottom[0], conv_top[1], conv_bottom[1])
            + conv_corner,
            small,
        )

        conv_out, mix_own, back_z2, ssm_block = tie(conv_out, mix_own, back_z2, ssm_block)
        gate_block = line_block(right((back_shard,))[0], right(back_z1), right(back_z2))
        gate_p1 = plane_first(gate_block)
        ssm_near, ssm_middle = line_first(ssm_block)
        mix_other = other_core(mix_own)
        count = groups // 2
        scanned = scan(0, count, conv_out, mix_own, mix_other, small)

        gate_p1, scanned, ssm_near, ssm_middle = tie(gate_p1, scanned, ssm_near, ssm_middle)
        gate_p2 = plane_second(gate_p1)
        crossed = along_z(ssm_near, Z_INNER)
        ends = along_z(ssm_middle, Z_ENDS)
        scanned = scan(
            count, groups - count, conv_out, mix_own, mix_other, small, (scanned,)
        )
        attn_block = line_block(left((back_shard,))[0], left(back_z1), left(back_z2))

        gate_p2, attn_block, scanned = tie(gate_p2, attn_block, scanned)
        attn_p1 = plane_first(attn_block)
        gated = gate(
            rows_own, rows_other, scanned, (gate_block,) + tuple(gate_p1) + tuple(gate_p2), 0
        )
        keep_early, send_early = ssm_out(gated, (1, 1), (ssm_block, ssm_near))

        attn_p1, keep_early, crossed, ends, ssm_near = tie(
            attn_p1, keep_early, crossed, ends, ssm_near
        )
        attn_p2 = plane_second(attn_p1)
        far = along_z(ssm_near, Z_FAR)
        got_early = other_core(send_early)
        attn_pieces = (attn_block,) + tuple(attn_p1) + tuple(attn_p2)
        heads = attention(rows_own, rows_other, attn_pieces, small[5])
        keep_attn, send_attn = attn_out(heads, attn_pieces)
        send_attn, far = tie(send_attn, far)
        got_attn = other_core(send_attn)
        attn = [keep_attn, got_attn]

        late_pieces = (ssm_middle, ends, crossed, far)
        keep_late, send_late = ssm_out(gated, (2, 2), late_pieces)
        got_late = other_core(send_late)
        ssm = [keep_early, got_early, keep_late, got_late]
        sums = squares(attn, ssm)
        other_sums = other_core(sums)
        received = []
        for part in range(pairs):
            mixed = mix(part, x_keep, attn, ssm, sums, other_sums, gains, features_back, small[6])
            received.append(
                (
                    mixed[0],
                    swap_x(mixed[1]),
                    swap_y(mixed[2]),
                    lax.ppermute(mixed[3], "rep", D_PAIRS),
                )
            )
        by_source = [jnp.stack([part[index] for part in received]) for index in range(rep_count)]
        for bit in (1, 2):
            swapped = (rep & bit) != 0
            by_source = [
                jnp.where(swapped, by_source[index ^ bit], by_source[index])
                for index in range(rep_count)
            ]
        mixed = jnp.concatenate(by_source, axis=0)
    else:

        def gathered(value):
            return lax.all_gather(value, ("rep", "tr"), axis=0, tiled=True)

        proc = group_order(serve_replica)
        small = small_operands(*plain)
        rows_own = spread(inverse_rms(tokens), rep, row)
        rows_other = other_core(rows_own)
        keep_pick, gains, features_back = column_picks(rep, row)
        x_keep = place(keep_pick)
        attn_pieces = (gathered(shard_behind(w_query, w_keyval, w_attn_out, w_inner[:, 1])),)
        heads = attention(rows_own, rows_other, attn_pieces, small[5])
        conv_out, mix_own = convolve(rows_own, rows_other, (gathered(conv_shard),), small)
        scanned = scan(0, groups, conv_out, mix_own, other_core(mix_own), small)
        gated = gate(rows_own, rows_other, scanned, attn_pieces, attn_width)
        keep_attn, send_attn = attn_out(heads, attn_pieces)
        attn = [keep_attn, other_core(send_attn)]
        kept, sent = ssm_out(gated, (1,), (gathered(ssm_shard),))
        ssm = [kept, other_core(sent)]
        sums = squares(attn, ssm)
        other_sums = other_core(sums)
        received = [
            jnp.stack(
                mix(part, x_keep, attn, ssm, sums, other_sums, gains, features_back, small[6])
            )
            for part in range(pairs)
        ]
        mixed = jnp.stack(received, axis=1).reshape(groups, group_rows, width)
        mixed = lax.all_to_all(mixed, "rep", split_axis=0, concat_axis=0, tiled=True)
    return mixed.reshape(groups, slots, steps, width)


def solution(mesh):
    placed = (
        P(("rep", "tr"), None, None, "tc"),
        P(("rep", "tr"), None, "tc"),
        P(("rep", "tr"), None, "tc"),
        P(("rep", "tr"), None, "tc"),
        P(),
        P(),
        P(),
        P("tc"),
        P(("rep", "tr"), "tc"),
        P(("rep", "tr"), "tc"),
        P(("rep", "tr"), None, "tc"),
        P(None, "tc"),
        P("tc"),
        P("tc", None),
        P(None, "tc"),
        P("tc"),
        P(None, "tc"),
        P("tc"),
        P("tc", ("rep", "tr")),
        P("tc", ("rep", "tr")),
        P(),
        P(),
    )
    return jax.shard_map(
        local,
        mesh=mesh,
        in_specs=placed,
        out_specs=P(("rep", "tr"), None, None, "tc"),
        check_vma=False,
    )
```

```python
import functools

import jax
import jax.numpy as jnp
from jax import lax
from jax.experimental import pallas as pl
from jax.experimental.pallas import tpu as pltpu
from jax.sharding import PartitionSpec as P

D = 1600
HD = 64
QH = 16
KVH = 4

EPSILON = 1e-06
LOG2_E = 1.4426950408889634

X_PAIRS = ((0, 1), (1, 0), (2, 3), (3, 2))
Y_PAIRS = ((0, 2), (2, 0), (1, 3), (3, 1))
D_PAIRS = ((0, 3), (3, 0), (1, 2), (2, 1))
Z_OUTER = ((0, 1), (1, 0), (2, 3), (3, 2))
Z_INNER = ((1, 2), (2, 1))
Z_ENDS = ((1, 0), (2, 3))
Z_FAR = ((2, 0), (1, 3))
Z_SLOTS = ((0, 1, 2, 3), (1, 0, 2, 3), (2, 3, 1, 0), (3, 2, 1, 0))

VMEM_LIMIT = 56 * 1024 * 1024


def params():
    return pltpu.CompilerParams(vmem_limit_bytes=VMEM_LIMIT)


def cost(flops, size):
    return pl.CostEstimate(flops=int(flops), bytes_accessed=int(size), transcendentals=0)


def tie(*values):
    return lax.optimization_barrier(values)


def swap_x(value):
    return lax.ppermute(value, "rep", X_PAIRS)


def swap_y(value):
    return lax.ppermute(value, "rep", Y_PAIRS)


def along_z(value, pairs):
    return lax.ppermute(value, "tr", pairs)


def other_core(value):
    return lax.ppermute(value, "tc", ((0, 1), (1, 0)))


def load_halves(pieces, target, sems, second, half, wide, column=0):
    width = target.shape[1]
    if wide > half:
        gap = jnp.zeros((wide - half, width), target.dtype)
        target[half:wide, :] = gap
        target[wide + half :, :] = gap
    copies = []
    start = 0
    for piece in pieces:
        count = piece.shape[0]
        for low in range(0, count, half):
            size = min(half, count)
            at_first = start < half
            place = (second if at_first else 1 - second) * wide + start % half
            copies.append(
                pltpu.make_async_copy(
                    piece.at[pl.ds(low, size), pl.ds(column, width)],
                    target.at[pl.ds(pl.multiple_of(place, 16), size), :],
                    sems.at[len(copies)],
                )
            )
            start += size
    for copy in copies:
        copy.start()
    for copy in copies:
        copy.wait()


def silu(value):
    scaled = 0.5 * value
    return scaled + scaled * jnp.tanh(scaled)


def row_mover(slots, steps, inward):
    count = slots * steps
    to_row = lax.broadcasted_iota(jnp.int32, (count, count), 0)
    from_row = lax.broadcasted_iota(jnp.int32, (count, count), 1)
    if inward:
        source = (to_row % slots) * steps + to_row // slots
    else:
        source = (to_row % steps) * slots + to_row // steps
    return jnp.where(from_row == source, 1.0, 0.0).astype(jnp.bfloat16)


def both_halves(rows_own, rows_other, weight):
    rows = jnp.concatenate([rows_own[...], rows_other[...]], axis=1)
    return jnp.dot(rows, weight[...], preferred_element_type=jnp.float32)


def exact_dot(left, right):
    return jnp.dot(left, right, preferred_element_type=jnp.float32).astype(jnp.bfloat16)


def spread_kernel(slots, proc, x, inv_rms, gain, pick, out):
    normed = (x[0].astype(jnp.float32) * inv_rms[0] * gain[...]).astype(jnp.bfloat16)
    mover = row_mover(slots, x.shape[1] // slots, True)
    out[...] = exact_dot(exact_dot(mover, normed), pick[...])


def place_kernel(slots, proc, x, pick, out):
    mover = row_mover(slots, x.shape[1] // slots, True)
    out[...] = exact_dot(exact_dot(mover, x[0]), pick[...])


def attention_kernel(
    slots,
    group_rows,
    kv_here,
    per_kv,
    count,
    half,
    first_column,
    proc,
    lengths,
    second,
    rows_own,
    rows_other,
    cache,
    *rest,
):
    pieces, (out, weight, sems) = rest[:count], rest[count:]
    tile = pl.program_id(0)

    @pl.when(tile == 0)
    def _():
        load_halves(pieces, weight, sems, second[0], half, weight.shape[0] // 2, first_column)

    made = both_halves(rows_own, rows_other, weight).astype(jnp.bfloat16)
    here = made.shape[0] // group_rows
    query_width = kv_here * per_kv * HD
    positions = cache.shape[1]
    stacked = per_kv * group_rows
    row_id = lax.broadcasted_iota(jnp.int32, (stacked, group_rows), 0) % group_rows
    column_id = lax.broadcasted_iota(jnp.int32, (stacked, group_rows), 1)
    own_mask = (row_id % slots == column_id % slots) & (column_id // slots <= row_id // slots)
    column = lax.broadcasted_iota(jnp.int32, (stacked, positions), 1)
    contract = (((1,), (1,)), ((), ()))
    scale = HD ** (-0.5)
    for index in range(here):
        group = proc[tile * here + index]
        prefix_mask = column < lengths[group]
        block = made[index * group_rows : (index + 1) * group_rows]
        past = cache[group]
        results = []
        for head in range(kv_here):
            query = jnp.concatenate(
                [
                    block[:, (head * per_kv + j) * HD : (head * per_kv + j + 1) * HD]
                    for j in range(per_kv)
                ],
                axis=0,
            )
            base = query_width + head * 2 * HD
            key_new = block[:, base : base + HD]
            value_new = block[:, base + HD : base + 2 * HD]
            key_old = past[:, head * 2 * HD : head * 2 * HD + HD]
            value_old = past[:, head * 2 * HD + HD : (head + 1) * 2 * HD]
            old = lax.dot_general(query, key_old, contract, preferred_element_type=jnp.float32)
            new = lax.dot_general(query, key_new, contract, preferred_element_type=jnp.float32)
            old = jnp.where(prefix_mask, old * scale, -jnp.inf)
            new = jnp.where(own_mask, new * scale, -jnp.inf)
            top = jnp.maximum(
                jnp.max(old, axis=1, keepdims=True), jnp.max(new, axis=1, keepdims=True)
            )
            old = jnp.exp(old - top)
            new = jnp.exp(new - top)
            total = jnp.sum(old, axis=1, keepdims=True) + jnp.sum(new, axis=1, keepdims=True)
            value = jnp.dot(
                old.astype(jnp.bfloat16), value_old, preferred_element_type=jnp.float32
            ) + jnp.dot(new.astype(jnp.bfloat16), value_new, preferred_element_type=jnp.float32)
            value = (value / total).astype(jnp.bfloat16)
            for j in range(per_kv):
                results.append(value[j * group_rows : (j + 1) * group_rows])
        out[index * group_rows : (index + 1) * group_rows, :] = jnp.concatenate(results, axis=1)


def conv_kernel(
    slots,
    group_rows,
    count,
    half,
    first_column,
    proc,
    second,
    rows_own,
    rows_other,
    history,
    taps,
    bias,
    mix_weight,
    *rest,
):
    pieces, (out, out_mix, weight, sems) = rest[:count], rest[count:]
    tile = pl.program_id(0)

    @pl.when(tile == 0)
    def _():
        load_halves(pieces, weight, sems, second[0], half, weight.shape[0] // 2, first_column)

    made = both_halves(rows_own, rows_other, weight)
    here = made.shape[0] // group_rows
    steps = group_rows // slots
    tap_count = taps.shape[0]
    past = history.shape[1]
    for index in range(here):
        start = index * group_rows
        state = history[proc[tile * here + index]]
        sequence = [
            jnp.broadcast_to(state[k : k + 1, :], (slots, made.shape[1])) for k in range(past)
        ] + [made[start + step * slots : start + (step + 1) * slots] for step in range(steps)]
        for step in range(steps):
            value = bias[...]
            for tap in range(tap_count):
                value = value + taps[tap : tap + 1, :] * sequence[step + tap]
            out[start + step * slots : start + (step + 1) * slots, :] = silu(value).astype(
                jnp.bfloat16
            )
    out_mix[...] = jnp.dot(
        out[...], mix_weight[...], preferred_element_type=jnp.float32
    ).astype(jnp.bfloat16)


def softplus(value):
    small = jnp.exp(-jnp.abs(value))
    series = small * (1.0 - small * (0.5 - small * (1.0 / 3.0)))
    return jnp.maximum(value, 0.0) + jnp.where(small < 0.01, series, jnp.log(1.0 + small))


def scan_kernel(
    slots, proc, conv, mix_own, mix_other, step_weight, step_bias, decay_log, skip, state, *rest
):
    out, *scratch = rest[-8:]
    step_scratch, drive_scratch, out_scratch, rate_scratch, state_scratch, in_mix, out_mix = scratch
    lanes = 128
    kind = jnp.bfloat16
    rank = step_weight.shape[0]
    states, channels = decay_log.shape
    total_rows = conv.shape[0]
    mix = mix_own[...].astype(jnp.float32) + mix_other[...].astype(jnp.float32)
    raw = (
        jnp.dot(mix[:, :rank].astype(kind), step_weight[...], preferred_element_type=jnp.float32)
        + step_bias[...]
    )
    step = softplus(raw)
    value = conv[...].astype(jnp.float32)
    step_scratch[:, :channels] = step
    drive_scratch[:, :channels] = step * value
    rate_scratch[:, :channels] = -jnp.exp(decay_log[...]) * LOG2_E
    state_scratch[:, :channels] = state[0]
    for n in range(states):
        in_mix[n] = jnp.broadcast_to(mix[:, 128 + n : 129 + n], (total_rows, lanes)).astype(kind)
        out_mix[n] = jnp.broadcast_to(
            mix[:, 128 + states + n : 129 + states + n], (total_rows, lanes)
        ).astype(kind)

    def one(chunk, carry):
        columns = pl.ds(pl.multiple_of(chunk * lanes, lanes), lanes)

        def spread(source, n):
            return jnp.broadcast_to(source[n : n + 1, columns], (slots, lanes)).astype(kind)

        held = [spread(state_scratch, n) for n in range(states)]
        for start in range(0, total_rows, slots):
            here = pl.ds(start, slots)
            size = step_scratch[here, columns].astype(kind)
            drive = drive_scratch[here, columns].astype(kind)
            total = None
            for first in range(0, states, 4):
                part = None
                for n in range(first, first + 4):
                    held[n] = (
                        jnp.exp2(size * spread(rate_scratch, n)) * held[n]
                        + drive * in_mix[n, here, :]
                    )
                    term = held[n] * out_mix[n, here, :]
                    part = term if part is None else part + term
                part = part.astype(jnp.float32)
                total = part if total is None else total + part
            out_scratch[here, columns] = total
        return carry

    lax.fori_loop(0, step_scratch.shape[1] // lanes, one, 0)
    out[...] = out_scratch[:, :channels] + skip[...] * value


def gate_kernel(count, half, first_column, second, rows_own, rows_other, scanned, *rest):
    pieces, (out, weight, sems) = rest[:count], rest[count:]

    @pl.when(pl.program_id(0) == 0)
    def _():
        load_halves(pieces, weight, sems, second[0], half, weight.shape[0] // 2, first_column)

    gate = both_halves(rows_own, rows_other, weight)
    out[...] = (scanned[...] * silu(gate)).astype(jnp.bfloat16)


def transposed_dot(left, right):
    return lax.dot_general(
        left, right, (((1,), (1,)), ((), ())), preferred_element_type=jnp.float32
    ).astype(jnp.bfloat16)


def attn_out_kernel(count, half, first_column, blocks, second, heads, *rest):
    pieces, (keep, send, raw, weight, sems) = rest[:count], rest[count:]
    wide = raw.shape[0] // 2
    columns = weight.shape[0] // 2

    @pl.when(pl.program_id(0) == 0)
    def _():
        load_halves(pieces, raw, sems, second[0], half, wide, first_column)
        loaded = raw[...].astype(jnp.float32)
        for index in range(2):
            parts = [
                jnp.zeros((size, loaded.shape[1]), jnp.float32)
                if at is None
                else loaded[index * wide + at : index * wide + at + size]
                for at, size in blocks
            ]
            weight[index * columns : (index + 1) * columns, :] = jnp.concatenate(
                parts, axis=0
            ).astype(weight.dtype)

    attended = heads[...]
    keep[...] = transposed_dot(attended, weight[:columns, :])
    send[...] = transposed_dot(attended, weight[columns:, :])


def ssm_out_kernel(slot_choices, part, scalars, gated, *rest):
    count = sum(slot_choices)
    pieces, (keep, send, weight, sems) = rest[:count], rest[count:]
    wide = weight.shape[0] // 2
    filled = part * len(slot_choices)
    second = scalars[0]

    @pl.when(pl.program_id(0) == 0)
    def _():
        if wide > filled:
            gap = jnp.zeros((wide - filled, weight.shape[1]), weight.dtype)
            weight[filled:wide, :] = gap
            weight[wide + filled :, :] = gap

        def copies(source, slot):
            for index, base in ((0, second), (1, 1 - second)):
                yield pltpu.make_async_copy(
                    source.at[pl.ds(pl.multiple_of(base * part, 16), part), :],
                    weight.at[pl.ds(index * wide + slot * part, part), :],
                    sems.at[slot, index],
                )

        at = 0
        firsts = []
        for slot, choices in enumerate(slot_choices):
            firsts.append(pieces[at])
            if choices == 1:
                for copy in copies(pieces[at], slot):
                    copy.start()
            else:
                for choice in range(2):

                    @pl.when(scalars[1] == 1 - choice)
                    def _(piece=pieces[at + choice], slot=slot):
                        for copy in copies(piece, slot):
                            copy.start()

            at += choices
        for slot, piece in enumerate(firsts):
            for copy in copies(piece, slot):
                copy.wait()

    value = gated[...]
    send[...] = transposed_dot(value, weight[wide:, :])
    keep[...] = transposed_dot(value, weight[:wide, :])


def square_sum(keep, got):
    value = keep[...].astype(jnp.float32) + got[...].astype(jnp.float32)
    return jnp.sum(value * value, axis=1, keepdims=True)


def square_kernel(*refs):
    *refs, out = refs
    out[:, 0:1] = square_sum(refs[0], refs[1])
    total = square_sum(refs[2], refs[3])
    for index in range(4, len(refs), 2):
        total += square_sum(refs[index], refs[index + 1])
    out[:, 1:2] = total


def mixed_kernel(slots, first, sections, here, proc, sizes, x_keep, keep_attn, got_attn, *rest):
    ssm_refs = rest[: 2 * sections]
    own_squares, other_squares, gains, features = rest[2 * sections : 2 * sections + 4]
    outs = rest[2 * sections + 4 : 2 * sections + 4 + here]
    made, sems = rest[2 * sections + 4 + here :]
    step = pl.program_id(0)
    ssm = jnp.concatenate(
        [
            keep[...].astype(jnp.float32) + got[...].astype(jnp.float32)
            for keep, got in zip(ssm_refs[::2], ssm_refs[1::2])
        ],
        axis=1,
    )
    attn = keep_attn[...].astype(jnp.float32) + got_attn[...].astype(jnp.float32)
    scales = lax.rsqrt((own_squares[...] + other_squares[...]) / D + EPSILON)
    branch = 0.5 * (
        gains[0:1, :] * attn * scales[:, 0:1] + gains[1:2, :] * ssm * scales[:, 1:2]
    )
    mixed = (x_keep[...].astype(jnp.float32) + branch).astype(jnp.bfloat16)
    placed = exact_dot(mixed, features[...])
    size = made.shape[1]
    in_step = mixed.shape[0] // size
    outward = row_mover(slots, size // slots, False)
    slot = lax.broadcasted_iota(jnp.int32, (size, 1), 0) // (size // slots)

    def copy(number):
        return pltpu.make_async_copy(made.at[number], outs[number], sems.at[number])

    for index in range(in_step):
        number = step * in_step + index
        rows = exact_dot(outward, placed[index * size : (index + 1) * size])
        live = slot < sizes[proc[first + number]]
        made[number] = jnp.where(live, rows, jnp.zeros_like(rows))
    for number in range(here):

        @pl.when(step == number // in_step)
        def _(number=number):
            copy(number).start()

    @pl.when(step == here // in_step - 1)
    def _():
        for number in range(here):
            copy(number).wait()


def local(
    tokens,
    prefix_kv,
    ssm_state,
    conv_state,
    prefix_len,
    group_size,
    serve_replica,
    in_gain,
    w_query,
    w_keyval,
    w_inner,
    conv_weight,
    conv_bias,
    w_xproj,
    dt_weight,
    dt_bias,
    decay_log,
    skip_gain,
    w_attn_out,
    w_ssm_out,
    attn_gain,
    ssm_gain,
):
    rep_count = lax.axis_size("rep")
    row_axis = lax.axis_size("tr")
    tensor_count = lax.axis_size("tc")
    rep = lax.axis_index("rep")
    row = lax.axis_index("tr")
    core = lax.axis_index("tc")
    groups, slots, steps, width = tokens.shape
    pairs = groups // rep_count
    kv_here = KVH // tensor_count
    per_kv = QH // KVH
    heads_width = QH // tensor_count * HD
    group_rows = slots * steps
    rows = groups * group_rows
    tile = groups // 4 * group_rows
    channels = w_inner.shape[2]
    shards = rep_count * row_axis
    shard = w_query.shape[0]
    pad = -(-shard // 8) * 8
    depth = shards * pad
    half = depth // 2
    wide = -(-half // 128) * 128
    by_links = rep_count == 4 and row_axis == 4
    sections = 2 if by_links else 1
    section = half // sections
    section_wide = -(-section // 128) * 128
    columns = sections * section_wide
    bf16 = jnp.bfloat16
    f32 = jnp.float32
    i32 = jnp.int32

    def padded(value):
        return jnp.pad(value, ((0, pad - shard), (0, 0)))

    ssm_shard = padded(w_ssm_out.T)
    conv_shard = padded(w_inner[:, 0])
    def shard_behind(w_query, w_keyval, w_attn_out, w_gate):
        return padded(jnp.concatenate([w_query, w_keyval, w_attn_out.T, w_gate], axis=1))

    qkv_width = w_query.shape[1] + w_keyval.shape[1]
    attn_width = qkv_width + heads_width
    rank, states = dt_weight.shape[0], decay_log.shape[0]
    mixes = 256

    def feature_at(column, lines_outside, rep, row):
        inside = column < half
        if lines_outside:
            inside = column % section_wide < section
            column = column // section_wide * section + column % section_wide
        block, offset = column // pad, column % pad
        if by_links:
            if lines_outside:
                slot, plane = block // 2, block % 2
            else:
                slot, plane = block % row_axis, block // row_axis
            low = row < 2
            line = jnp.where(
                slot == 0,
                row,
                jnp.where(
                    slot == 1,
                    row ^ 1,
                    jnp.where(slot == 2, jnp.where(low, 2, 1), jnp.where(low, 3, 0)),
                ),
            )
            block = ((rep % 2) ^ plane) * row_axis + line
        return jnp.where((offset < shard) & inside, block * shard + offset, -1)

    def picker(shape, column_dim, lines_outside, rep, row):
        line = tuple(size if dim == column_dim else 1 for dim, size in enumerate(shape))
        column = lax.broadcasted_iota(i32, line, column_dim)
        (source,) = tie(feature_at(column, lines_outside, rep, row))
        return lax.broadcasted_iota(i32, shape, 1 - column_dim) == source

    def column_picks(rep, row):
        keep_pick = picker((width, columns), 1, True, rep, row)
        gains = jnp.stack([attn_gain, ssm_gain])
        gains = lax.dynamic_slice_in_dim(gains, core * width, width, 1)
        gains = jnp.sum(jnp.where(keep_pick[None], gains[:, :, None], 0.0), axis=1)
        features_back = picker((columns, width), 0, True, rep, row).astype(bf16)
        return keep_pick.astype(bf16), gains, features_back

    second = ((rep // 2) ^ core if by_links else core).astype(i32)[None]

    def group_order(serve_replica):
        served = lax.dynamic_slice_in_dim(serve_replica, first_group, groups, 0)
        target = served ^ rep if by_links else served
        ids = jnp.arange(groups, dtype=i32)
        same = (served[:, None] == served[None, :]) & (ids[None, :] < ids[:, None])
        places = jnp.sum(same.astype(i32), axis=1) * rep_count + target
        return jnp.sum(
            jnp.where(places[None, :] == ids[:, None], ids[None, :], 0), axis=1
        ).astype(i32)

    def inverse_rms(tokens):
        wide_rows = tokens.reshape(groups, group_rows, width).astype(f32)
        square_sums = lax.psum(jnp.sum(wide_rows * wide_rows, axis=2), "tc")
        return lax.rsqrt(square_sums / D + EPSILON)[:, :, None]

    first_group = (rep * row_axis + row) * groups
    def row_block(columns, size=tile, first=0):
        return pl.BlockSpec((size, columns), lambda g, *_: (g + first, 0))

    def whole(*shape):
        return pl.BlockSpec(shape, lambda g, *_: (0,) * len(shape))

    def group_block(*shape, first=0):
        return pl.BlockSpec(
            (1,) + shape, lambda g, proc, *_: (proc[g + first],) + (0,) * len(shape)
        )

    anywhere = pl.BlockSpec(memory_space=pl.ANY)

    def rows_of(columns, kind=bf16, count=rows):
        return jax.ShapeDtypeStruct((count, columns), kind)

    def call(kernel, scalars, grid, in_specs, out_specs, out_shape, scratch, spend, name, alias=None):
        return pl.pallas_call(
            kernel,
            grid_spec=pltpu.PrefetchScalarGridSpec(
                num_scalar_prefetch=scalars,
                grid=(grid,),
                in_specs=in_specs,
                out_specs=out_specs,
                scratch_shapes=scratch,
            ),
            out_shape=out_shape,
            input_output_aliases=alias or {},
            compiler_params=params(),
            cost_estimate=cost(spend * 1.0e7, rows * 4),
            name=name,
        )

    def piece_copies(pieces):
        return pltpu.SemaphoreType.DMA((max(len(pieces), 2),))

    def spread(inv, rep, row):
        spread_pick = picker((width, wide), 1, False, rep, row).astype(bf16)
        return call(
            functools.partial(spread_kernel, slots),
            1,
            groups,
            [
                group_block(group_rows, width),
                group_block(group_rows, 1),
                whole(1, width),
                whole(width, wide),
            ],
            row_block(wide, group_rows),
            rows_of(wide),
            [],
            8,
            "spread_rows",
        )(proc, tokens.reshape(groups, group_rows, width), inv, in_gain[None], spread_pick)

    def place(keep_pick):
        return call(
            functools.partial(place_kernel, slots),
            1,
            groups,
            [group_block(group_rows, width), whole(width, columns)],
            row_block(columns, group_rows),
            rows_of(columns),
            [],
            8,
            "place_rows",
        )(proc, tokens.reshape(groups, group_rows, width), keep_pick)

    def attention(rows_own, rows_other, pieces, lengths):
        return call(
            functools.partial(
                attention_kernel, slots, group_rows, kv_here, per_kv, len(pieces), half, 0
            ),
            3,
            rows // tile,
            [row_block(wide)] * 2 + [whole(*prefix_kv.shape)] + [anywhere] * len(pieces),
            row_block(heads_width),
            rows_of(heads_width),
            [pltpu.VMEM((2 * wide, qkv_width), bf16), piece_copies(pieces)],
            15,
            "attention",
        )(proc, lengths, second, rows_own, rows_other, prefix_kv, *pieces)

    def small_operands(w_xproj, conv_state, conv_bias, dt_bias, skip_gain, prefix_len, group_size):
        mix_weight = jnp.concatenate(
            [
                jnp.pad(w_xproj[:, :rank], ((0, 0), (0, 128 - rank))),
                jnp.pad(w_xproj[:, rank:], ((0, 0), (0, mixes - 128 - 2 * states))),
            ],
            axis=1,
        )
        return (
            mix_weight,
            conv_state,
            conv_bias[None],
            dt_bias[None],
            skip_gain[None],
            lax.dynamic_slice_in_dim(prefix_len, first_group, groups, 0),
            lax.dynamic_slice_in_dim(group_size, first_group, groups, 0),
        )

    plain = (w_xproj, conv_state, conv_bias, dt_bias, skip_gain, prefix_len, group_size)

    def convolve(rows_own, rows_other, pieces, small):
        return call(
            functools.partial(conv_kernel, slots, group_rows, len(pieces), half, 0),
            2,
            rows // tile,
            [
                row_block(wide),
                row_block(wide),
                whole(*conv_state.shape),
                whole(*conv_weight.shape),
                whole(1, channels),
                whole(channels, mixes),
            ]
            + [anywhere] * len(pieces),
            [row_block(channels), row_block(mixes)],
            [rows_of(channels), rows_of(mixes)],
            [pltpu.VMEM((2 * wide, channels), bf16), piece_copies(pieces)],
            14,
            "convolve",
        )(
            proc,
            second,
            rows_own,
            rows_other,
            small[1],
            conv_weight,
            small[2],
            small[0],
            *pieces,
        )

    def scan(first, count, conv_out, mix_own, mix_other, small, earlier=()):
        across = -(-channels // 128) * 128
        blocks = functools.partial(row_block, size=group_rows, first=first)
        return call(
            functools.partial(scan_kernel, slots),
            1,
            count,
            [
                blocks(channels),
                blocks(mixes),
                blocks(mixes),
                whole(rank, channels),
                whole(1, channels),
                whole(states, channels),
                whole(1, channels),
                group_block(*ssm_state.shape[1:], first=first),
            ]
            + [anywhere] * len(earlier),
            blocks(channels),
            rows_of(channels, f32),
            [pltpu.VMEM((group_rows, across), f32)] * 3
            + [pltpu.VMEM((states, across), f32)] * 2
            + [pltpu.VMEM((states, group_rows, 128), bf16)] * 2,
            4 * count,
            "scan_states",
            {9: 0} if earlier else None,
        )(
            proc,
            conv_out,
            mix_own,
            mix_other,
            dt_weight,
            small[3],
            decay_log,
            small[4],
            ssm_state,
            *earlier,
        )

    def gate(rows_own, rows_other, scanned, pieces, first_column):
        return call(
            functools.partial(gate_kernel, len(pieces), half, first_column),
            1,
            rows // tile,
            [row_block(wide)] * 2 + [row_block(channels)] + [anywhere] * len(pieces),
            row_block(channels),
            rows_of(channels),
            [pltpu.VMEM((2 * wide, channels), bf16), piece_copies(pieces)],
            13,
            "gate",
        )(second, rows_own, rows_other, scanned, *pieces)

    def attn_out(heads, pieces):
        blocks = []
        for number in range(sections):
            if by_links:
                blocks += [
                    ((plane * row_axis + slot) * pad, pad)
                    for slot in (2 * number, 2 * number + 1)
                    for plane in range(2)
                ]
            else:
                blocks.append((0, half))
            if section_wide > section:
                blocks.append((None, section_wide - section))
        return call(
            functools.partial(attn_out_kernel, len(pieces), half, qkv_width, tuple(blocks)),
            1,
            rows // tile,
            [row_block(heads_width)] + [anywhere] * len(pieces),
            [row_block(columns)] * 2,
            [rows_of(columns)] * 2,
            [
                pltpu.VMEM((2 * wide, heads_width), bf16),
                pltpu.VMEM((2 * columns, heads_width), bf16),
                piece_copies(pieces),
            ],
            6,
            "attn_out",
        )(second, heads, *pieces)

    def ssm_out(gated, choices, pieces):
        scalars = jnp.stack([second[0], inner.astype(i32) if by_links else second[0]])
        return call(
            functools.partial(ssm_out_kernel, choices, section // len(choices)),
            1,
            rows // tile,
            [row_block(channels)] + [anywhere] * len(pieces),
            [row_block(section_wide)] * 2,
            [rows_of(section_wide)] * 2,
            [
                pltpu.VMEM((2 * section_wide, channels), bf16),
                pltpu.SemaphoreType.DMA((len(choices), 2)),
            ],
            8,
            "ssm_out",
        )(scalars, gated, *pieces)

    def squares(attn, ssm):
        return call(
            square_kernel,
            0,
            rows // tile,
            [row_block(columns)] * 2 + [row_block(section_wide)] * len(ssm),
            row_block(2),
            rows_of(2, f32),
            [],
            2,
            "squares",
        )(*attn, *ssm)

    def mix(part, x_keep, attn, ssm, own_squares, other_squares, gains, features_back, sizes):
        here = groups // pairs
        size = 2 * group_rows
        block = functools.partial(row_block, size=size, first=part * here // 2)
        return call(
            functools.partial(mixed_kernel, slots, part * here, sections, here),
            2,
            here // 2,
            [block(columns)] * 3
            + [block(section_wide)] * (2 * sections)
            + [block(2)] * 2
            + [whole(2, columns), whole(columns, width)],
            [anywhere] * here,
            [rows_of(width, count=group_rows)] * here,
            [pltpu.VMEM((here, group_rows, width), bf16), pltpu.SemaphoreType.DMA((here,))],
            4,
            "mixed_rows",
        )(
            proc,
            sizes,
            x_keep,
            *attn,
            *ssm,
            own_squares,
            other_squares,
            gains,
            features_back,
        )

    if by_links:

        def line_first(value):
            return along_z(value, Z_OUTER), along_z(value, Z_INNER)

        def line_second(first):
            near, middle = first
            return along_z(near, Z_INNER), along_z(middle, Z_ENDS), along_z(near, Z_FAR)

        inner = (row == 1) | (row == 2)

        def line_block(value, first, last):
            near, middle = first
            crossed, ends, far = last
            return jnp.concatenate(
                [value, near, jnp.where(inner, middle, ends), jnp.where(inner, crossed, far)],
                axis=0,
            )

        def plane_first(value):
            return swap_x(value), swap_y(value)

        def plane_second(first):
            by_x, by_y = first
            cut = by_x.shape[0] // 16 * 8
            return swap_y(by_x[:cut]), swap_x(by_y[cut:])

        def upper(value, first):
            return jnp.concatenate([value, first[0]], axis=0)

        def lower(first, last):
            crossed, ends, far = last
            return jnp.concatenate(
                [jnp.where(inner, first[1], ends), jnp.where(inner, crossed, far)], axis=0
            )

        def left(values):
            return tuple(value[:, :attn_width] for value in values)

        def right(values):
            return tuple(value[:, attn_width:] for value in values)

        ssm_corner = lax.ppermute(ssm_shard, "rep", D_PAIRS)
        ssm_late, conv_shard = tie(ssm_shard, conv_shard)
        ssm_plane = plane_first(ssm_late) + (ssm_corner,)
        conv_z1 = line_first(conv_shard)
        inv_rms = inverse_rms(tokens)

        (
            conv_z1,
            conv_shard,
            ssm_plane,
            inv_rms,
            serve_late,
            rep_late,
            row_late,
            late_weights,
        ) = tie(
            conv_z1,
            conv_shard,
            ssm_plane,
            inv_rms,
            serve_replica,
            rep,
            row,
            (w_query, w_keyval, w_attn_out, w_inner[:, 1]),
        )
        conv_z2 = line_second(conv_z1)
        conv_top_own = upper(conv_shard, conv_z1)
        conv_top = plane_first(conv_top_own)
        proc = group_order(serve_late)
        rows_own = spread(inv_rms, rep_late, row_late)
        back_shard = shard_behind(*late_weights)

        conv_bottom_own = lower(conv_z1, conv_z2)
        conv_top, conv_bottom_own, back_shard, rows_own, plain, rep_late, row_late = tie(
            conv_top, conv_bottom_own, back_shard, rows_own, plain, rep, row
        )
        conv_bottom = plane_first(conv_bottom_own)
        back_z1 = line_first(back_shard)
        rows_other = other_core(rows_own)
        small = small_operands(*plain)
        picks = column_picks(rep_late, row_late)

        conv_top, conv_bottom, back_z1, small, rows_other, ssm_plane, picks = tie(
            conv_top, conv_bottom, back_z1, small, rows_other, ssm_plane, picks
        )
        keep_pick, gains, features_back = picks
        conv_corner = (swap_y(conv_top[0]), swap_x(conv_bottom[1]))
        back_z2 = line_second(back_z1)
        ssm_block = jnp.concatenate((ssm_shard,) + ssm_plane, axis=0)
        x_keep = place(keep_pick)

        conv_corner, ssm_block, x_keep, gains, features_back = tie(
            conv_corner, ssm_block, x_keep, gains, features_back
        )
        conv_out, mix_own = convolve(
            rows_own,
            rows_other,
            (conv_top_own, conv_bottom_own, conv_top[0], conv_bottom[0], conv_top[1], conv_bottom[1])
            + conv_corner,
            small,
        )

        conv_out, mix_own, back_z2, ssm_block = tie(conv_out, mix_own, back_z2, ssm_block)
        gate_block = line_block(right((back_shard,))[0], right(back_z1), right(back_z2))
        gate_p1 = plane_first(gate_block)
        ssm_near, ssm_middle = line_first(ssm_block)
        mix_other = other_core(mix_own)
        count = groups // 2
        scanned = scan(0, count, conv_out, mix_own, mix_other, small)

        gate_p1, scanned = tie(gate_p1, scanned)
        gate_p2 = plane_second(gate_p1)
        quarter = groups // 4
        scanned = scan(count, quarter, conv_out, mix_own, mix_other, small, (scanned,))
        scanned, ssm_near, ssm_middle = tie(scanned, ssm_near, ssm_middle)
        crossed = along_z(ssm_near, Z_INNER)
        ends = along_z(ssm_middle, Z_ENDS)
        scanned = scan(
            count + quarter, quarter, conv_out, mix_own, mix_other, small, (scanned,)
        )
        attn_block = line_block(left((back_shard,))[0], left(back_z1), left(back_z2))

        gate_p2, attn_block, scanned = tie(gate_p2, attn_block, scanned)
        attn_p1 = plane_first(attn_block)
        gated = gate(
            rows_own, rows_other, scanned, (gate_block,) + tuple(gate_p1) + tuple(gate_p2), 0
        )
        keep_early, send_early = ssm_out(gated, (1, 1), (ssm_block, ssm_near))

        attn_p1, keep_early, crossed, ends, ssm_near = tie(
            attn_p1, keep_early, crossed, ends, ssm_near
        )
        attn_p2 = plane_second(attn_p1)
        far = along_z(ssm_near, Z_FAR)
        got_early = other_core(send_early)
        attn_pieces = (attn_block,) + tuple(attn_p1) + tuple(attn_p2)
        heads = attention(rows_own, rows_other, attn_pieces, small[5])
        keep_attn, send_attn = attn_out(heads, attn_pieces)
        send_attn, far = tie(send_attn, far)
        got_attn = other_core(send_attn)
        attn = [keep_attn, got_attn]

        late_pieces = (ssm_middle, ends, crossed, far)
        keep_late, send_late = ssm_out(gated, (2, 2), late_pieces)
        got_late = other_core(send_late)
        ssm = [keep_early, got_early, keep_late, got_late]
        sums = squares(attn, ssm)
        other_sums = other_core(sums)
        received = []
        for part in range(pairs):
            mixed = mix(part, x_keep, attn, ssm, sums, other_sums, gains, features_back, small[6])
            received.append(
                (
                    mixed[0],
                    swap_x(mixed[1]),
                    swap_y(mixed[2]),
                    lax.ppermute(mixed[3], "rep", D_PAIRS),
                )
            )
        by_source = [jnp.stack([part[index] for part in received]) for index in range(rep_count)]
        for bit in (1, 2):
            swapped = (rep & bit) != 0
            by_source = [
                jnp.where(swapped, by_source[index ^ bit], by_source[index])
                for index in range(rep_count)
            ]
        mixed = jnp.concatenate(by_source, axis=0)
    else:

        def gathered(value):
            return lax.all_gather(value, ("rep", "tr"), axis=0, tiled=True)

        proc = group_order(serve_replica)
        small = small_operands(*plain)
        rows_own = spread(inverse_rms(tokens), rep, row)
        rows_other = other_core(rows_own)
        keep_pick, gains, features_back = column_picks(rep, row)
        x_keep = place(keep_pick)
        attn_pieces = (gathered(shard_behind(w_query, w_keyval, w_attn_out, w_inner[:, 1])),)
        heads = attention(rows_own, rows_other, attn_pieces, small[5])
        conv_out, mix_own = convolve(rows_own, rows_other, (gathered(conv_shard),), small)
        scanned = scan(0, groups, conv_out, mix_own, other_core(mix_own), small)
        gated = gate(rows_own, rows_other, scanned, attn_pieces, attn_width)
        keep_attn, send_attn = attn_out(heads, attn_pieces)
        attn = [keep_attn, other_core(send_attn)]
        kept, sent = ssm_out(gated, (1,), (gathered(ssm_shard),))
        ssm = [kept, other_core(sent)]
        sums = squares(attn, ssm)
        other_sums = other_core(sums)
        received = [
            jnp.stack(
                mix(part, x_keep, attn, ssm, sums, other_sums, gains, features_back, small[6])
            )
            for part in range(pairs)
        ]
        mixed = jnp.stack(received, axis=1).reshape(groups, group_rows, width)
        mixed = lax.all_to_all(mixed, "rep", split_axis=0, concat_axis=0, tiled=True)
    return mixed.reshape(groups, slots, steps, width)


def solution(mesh):
    placed = (
        P(("rep", "tr"), None, None, "tc"),
        P(("rep", "tr"), None, "tc"),
        P(("rep", "tr"), None, "tc"),
        P(("rep", "tr"), None, "tc"),
        P(),
        P(),
        P(),
        P("tc"),
        P(("rep", "tr"), "tc"),
        P(("rep", "tr"), "tc"),
        P(("rep", "tr"), None, "tc"),
        P(None, "tc"),
        P("tc"),
        P("tc", None),
        P(None, "tc"),
        P("tc"),
        P(None, "tc"),
        P("tc"),
        P("tc", ("rep", "tr")),
        P("tc", ("rep", "tr")),
        P(),
        P(),
    )
    return jax.shard_map(
        local,
        mesh=mesh,
        in_specs=placed,
        out_specs=P(("rep", "tr"), None, None, "tc"),
        check_vma=False,
    )
```

```python
import functools

import jax
import jax.numpy as jnp
from jax import lax
from jax.experimental import pallas as pl
from jax.experimental.pallas import tpu as pltpu
from jax.sharding import PartitionSpec as P

D = 1600
HD = 64
QH = 16
KVH = 4

EPSILON = 1e-06
LOG2_E = 1.4426950408889634

X_PAIRS = ((0, 1), (1, 0), (2, 3), (3, 2))
Y_PAIRS = ((0, 2), (2, 0), (1, 3), (3, 1))
D_PAIRS = ((0, 3), (3, 0), (1, 2), (2, 1))
Z_OUTER = ((0, 1), (1, 0), (2, 3), (3, 2))
Z_INNER = ((1, 2), (2, 1))
Z_ENDS = ((1, 0), (2, 3))
Z_FAR = ((2, 0), (1, 3))
Z_SLOTS = ((0, 1, 2, 3), (1, 0, 2, 3), (2, 3, 1, 0), (3, 2, 1, 0))

VMEM_LIMIT = 56 * 1024 * 1024


def params():
    return pltpu.CompilerParams(vmem_limit_bytes=VMEM_LIMIT)


def cost(flops, size):
    return pl.CostEstimate(flops=int(flops), bytes_accessed=int(size), transcendentals=0)


def tie(*values):
    return lax.optimization_barrier(values)


def swap_x(value):
    return lax.ppermute(value, "rep", X_PAIRS)


def swap_y(value):
    return lax.ppermute(value, "rep", Y_PAIRS)


def along_z(value, pairs):
    return lax.ppermute(value, "tr", pairs)


def other_core(value):
    return lax.ppermute(value, "tc", ((0, 1), (1, 0)))


def load_halves(pieces, target, sems, second, half, wide, column=0):
    width = target.shape[1]
    if wide > half:
        gap = jnp.zeros((wide - half, width), target.dtype)
        target[half:wide, :] = gap
        target[wide + half :, :] = gap
    copies = []
    start = 0
    for piece in pieces:
        count = piece.shape[0]
        for low in range(0, count, half):
            size = min(half, count)
            at_first = start < half
            place = (second if at_first else 1 - second) * wide + start % half
            copies.append(
                pltpu.make_async_copy(
                    piece.at[pl.ds(low, size), pl.ds(column, width)],
                    target.at[pl.ds(pl.multiple_of(place, 16), size), :],
                    sems.at[len(copies)],
                )
            )
            start += size
    for copy in copies:
        copy.start()
    for copy in copies:
        copy.wait()


def silu(value):
    scaled = 0.5 * value
    return scaled + scaled * jnp.tanh(scaled)


def row_mover(slots, steps, inward):
    count = slots * steps
    to_row = lax.broadcasted_iota(jnp.int32, (count, count), 0)
    from_row = lax.broadcasted_iota(jnp.int32, (count, count), 1)
    if inward:
        source = (to_row % slots) * steps + to_row // slots
    else:
        source = (to_row % steps) * slots + to_row // steps
    return jnp.where(from_row == source, 1.0, 0.0).astype(jnp.bfloat16)


def both_halves(rows_own, rows_other, weight):
    rows = jnp.concatenate([rows_own[...], rows_other[...]], axis=1)
    return jnp.dot(rows, weight[...], preferred_element_type=jnp.float32)


def exact_dot(left, right):
    return jnp.dot(left, right, preferred_element_type=jnp.float32).astype(jnp.bfloat16)


def spread_kernel(slots, proc, x, inv_rms, gain, pick, out):
    normed = (x[0].astype(jnp.float32) * inv_rms[0] * gain[...]).astype(jnp.bfloat16)
    mover = row_mover(slots, x.shape[1] // slots, True)
    out[...] = exact_dot(exact_dot(mover, normed), pick[...])


def place_kernel(slots, proc, x, pick, out):
    mover = row_mover(slots, x.shape[1] // slots, True)
    out[...] = exact_dot(exact_dot(mover, x[0]), pick[...])


def attention_kernel(
    slots,
    group_rows,
    kv_here,
    per_kv,
    count,
    half,
    first_column,
    proc,
    lengths,
    second,
    rows_own,
    rows_other,
    cache,
    *rest,
):
    pieces, (out, weight, sems) = rest[:count], rest[count:]
    tile = pl.program_id(0)

    @pl.when(tile == 0)
    def _():
        load_halves(pieces, weight, sems, second[0], half, weight.shape[0] // 2, first_column)

    made = both_halves(rows_own, rows_other, weight).astype(jnp.bfloat16)
    here = made.shape[0] // group_rows
    query_width = kv_here * per_kv * HD
    positions = cache.shape[1]
    stacked = per_kv * group_rows
    row_id = lax.broadcasted_iota(jnp.int32, (stacked, group_rows), 0) % group_rows
    column_id = lax.broadcasted_iota(jnp.int32, (stacked, group_rows), 1)
    own_mask = (row_id % slots == column_id % slots) & (column_id // slots <= row_id // slots)
    column = lax.broadcasted_iota(jnp.int32, (stacked, positions), 1)
    contract = (((1,), (1,)), ((), ()))
    scale = HD ** (-0.5)
    for index in range(here):
        group = proc[tile * here + index]
        prefix_mask = column < lengths[group]
        block = made[index * group_rows : (index + 1) * group_rows]
        past = cache[group]
        results = []
        for head in range(kv_here):
            query = jnp.concatenate(
                [
                    block[:, (head * per_kv + j) * HD : (head * per_kv + j + 1) * HD]
                    for j in range(per_kv)
                ],
                axis=0,
            )
            base = query_width + head * 2 * HD
            key_new = block[:, base : base + HD]
            value_new = block[:, base + HD : base + 2 * HD]
            key_old = past[:, head * 2 * HD : head * 2 * HD + HD]
            value_old = past[:, head * 2 * HD + HD : (head + 1) * 2 * HD]
            old = lax.dot_general(query, key_old, contract, preferred_element_type=jnp.float32)
            new = lax.dot_general(query, key_new, contract, preferred_element_type=jnp.float32)
            old = jnp.where(prefix_mask, old * scale, -jnp.inf)
            new = jnp.where(own_mask, new * scale, -jnp.inf)
            top = jnp.maximum(
                jnp.max(old, axis=1, keepdims=True), jnp.max(new, axis=1, keepdims=True)
            )
            old = jnp.exp(old - top)
            new = jnp.exp(new - top)
            total = jnp.sum(old, axis=1, keepdims=True) + jnp.sum(new, axis=1, keepdims=True)
            value = jnp.dot(
                old.astype(jnp.bfloat16), value_old, preferred_element_type=jnp.float32
            ) + jnp.dot(new.astype(jnp.bfloat16), value_new, preferred_element_type=jnp.float32)
            value = (value / total).astype(jnp.bfloat16)
            for j in range(per_kv):
                results.append(value[j * group_rows : (j + 1) * group_rows])
        out[index * group_rows : (index + 1) * group_rows, :] = jnp.concatenate(results, axis=1)


def conv_kernel(
    slots,
    group_rows,
    count,
    half,
    first_column,
    proc,
    second,
    rows_own,
    rows_other,
    history,
    taps,
    bias,
    mix_weight,
    *rest,
):
    pieces, (out, out_mix, weight, sems) = rest[:count], rest[count:]
    tile = pl.program_id(0)

    @pl.when(tile == 0)
    def _():
        load_halves(pieces, weight, sems, second[0], half, weight.shape[0] // 2, first_column)

    made = both_halves(rows_own, rows_other, weight)
    here = made.shape[0] // group_rows
    steps = group_rows // slots
    tap_count = taps.shape[0]
    past = history.shape[1]
    for index in range(here):
        start = index * group_rows
        state = history[proc[tile * here + index]]
        sequence = [
            jnp.broadcast_to(state[k : k + 1, :], (slots, made.shape[1])) for k in range(past)
        ] + [made[start + step * slots : start + (step + 1) * slots] for step in range(steps)]
        for step in range(steps):
            value = bias[...]
            for tap in range(tap_count):
                value = value + taps[tap : tap + 1, :] * sequence[step + tap]
            out[start + step * slots : start + (step + 1) * slots, :] = silu(value).astype(
                jnp.bfloat16
            )
    out_mix[...] = jnp.dot(
        out[...], mix_weight[...], preferred_element_type=jnp.float32
    ).astype(jnp.bfloat16)


def softplus(value):
    small = jnp.exp(-jnp.abs(value))
    series = small * (1.0 - small * (0.5 - small * (1.0 / 3.0)))
    return jnp.maximum(value, 0.0) + jnp.where(small < 0.01, series, jnp.log(1.0 + small))


def scan_kernel(
    slots, proc, conv, mix_own, mix_other, step_weight, step_bias, decay_log, skip, state, *rest
):
    out, *scratch = rest[-8:]
    step_scratch, drive_scratch, out_scratch, rate_scratch, state_scratch, in_mix, out_mix = scratch
    lanes = 128
    kind = jnp.bfloat16
    rank = step_weight.shape[0]
    states, channels = decay_log.shape
    total_rows = conv.shape[0]
    mix = mix_own[...].astype(jnp.float32) + mix_other[...].astype(jnp.float32)
    raw = (
        jnp.dot(mix[:, :rank].astype(kind), step_weight[...], preferred_element_type=jnp.float32)
        + step_bias[...]
    )
    step = softplus(raw)
    value = conv[...].astype(jnp.float32)
    step_scratch[:, :channels] = step
    drive_scratch[:, :channels] = step * value
    rate_scratch[:, :channels] = -jnp.exp(decay_log[...]) * LOG2_E
    state_scratch[:, :channels] = state[0]
    for n in range(states):
        in_mix[n] = jnp.broadcast_to(mix[:, 128 + n : 129 + n], (total_rows, lanes)).astype(kind)
        out_mix[n] = jnp.broadcast_to(
            mix[:, 128 + states + n : 129 + states + n], (total_rows, lanes)
        ).astype(kind)

    def one(chunk, carry):
        columns = pl.ds(pl.multiple_of(chunk * lanes, lanes), lanes)

        def spread(source, n):
            return jnp.broadcast_to(source[n : n + 1, columns], (slots, lanes)).astype(kind)

        held = [spread(state_scratch, n) for n in range(states)]
        for start in range(0, total_rows, slots):
            here = pl.ds(start, slots)
            size = step_scratch[here, columns].astype(kind)
            drive = drive_scratch[here, columns].astype(kind)
            total = None
            for first in range(0, states, 4):
                part = None
                for n in range(first, first + 4):
                    held[n] = (
                        jnp.exp2(size * spread(rate_scratch, n)) * held[n]
                        + drive * in_mix[n, here, :]
                    )
                    term = held[n] * out_mix[n, here, :]
                    part = term if part is None else part + term
                part = part.astype(jnp.float32)
                total = part if total is None else total + part
            out_scratch[here, columns] = total
        return carry

    lax.fori_loop(0, step_scratch.shape[1] // lanes, one, 0)
    out[...] = out_scratch[:, :channels] + skip[...] * value


def gate_kernel(count, half, first_column, second, rows_own, rows_other, scanned, *rest):
    pieces, (out, weight, sems) = rest[:count], rest[count:]

    @pl.when(pl.program_id(0) == 0)
    def _():
        load_halves(pieces, weight, sems, second[0], half, weight.shape[0] // 2, first_column)

    gate = both_halves(rows_own, rows_other, weight)
    out[...] = (scanned[...] * silu(gate)).astype(jnp.bfloat16)


def transposed_dot(left, right):
    return lax.dot_general(
        left, right, (((1,), (1,)), ((), ())), preferred_element_type=jnp.float32
    ).astype(jnp.bfloat16)


def attn_out_kernel(count, half, first_column, blocks, second, heads, *rest):
    pieces, (keep, send, raw, weight, sems) = rest[:count], rest[count:]
    wide = raw.shape[0] // 2
    columns = weight.shape[0] // 2

    @pl.when(pl.program_id(0) == 0)
    def _():
        load_halves(pieces, raw, sems, second[0], half, wide, first_column)
        loaded = raw[...].astype(jnp.float32)
        for index in range(2):
            parts = [
                jnp.zeros((size, loaded.shape[1]), jnp.float32)
                if at is None
                else loaded[index * wide + at : index * wide + at + size]
                for at, size in blocks
            ]
            weight[index * columns : (index + 1) * columns, :] = jnp.concatenate(
                parts, axis=0
            ).astype(weight.dtype)

    attended = heads[...]
    keep[...] = transposed_dot(attended, weight[:columns, :])
    send[...] = transposed_dot(attended, weight[columns:, :])


def ssm_out_kernel(slot_choices, part, scalars, gated, *rest):
    count = sum(slot_choices)
    pieces, (keep, send, weight, sems) = rest[:count], rest[count:]
    wide = weight.shape[0] // 2
    filled = part * len(slot_choices)
    second = scalars[0]

    @pl.when(pl.program_id(0) == 0)
    def _():
        if wide > filled:
            gap = jnp.zeros((wide - filled, weight.shape[1]), weight.dtype)
            weight[filled:wide, :] = gap
            weight[wide + filled :, :] = gap

        def copies(source, slot):
            for index, base in ((0, second), (1, 1 - second)):
                yield pltpu.make_async_copy(
                    source.at[pl.ds(pl.multiple_of(base * part, 16), part), :],
                    weight.at[pl.ds(index * wide + slot * part, part), :],
                    sems.at[slot, index],
                )

        at = 0
        firsts = []
        for slot, choices in enumerate(slot_choices):
            firsts.append(pieces[at])
            if choices == 1:
                for copy in copies(pieces[at], slot):
                    copy.start()
            else:
                for choice in range(2):

                    @pl.when(scalars[1] == 1 - choice)
                    def _(piece=pieces[at + choice], slot=slot):
                        for copy in copies(piece, slot):
                            copy.start()

            at += choices
        for slot, piece in enumerate(firsts):
            for copy in copies(piece, slot):
                copy.wait()

    value = gated[...]
    send[...] = transposed_dot(value, weight[wide:, :])
    keep[...] = transposed_dot(value, weight[:wide, :])


def square_sum(keep, got):
    value = keep[...].astype(jnp.float32) + got[...].astype(jnp.float32)
    return jnp.sum(value * value, axis=1, keepdims=True)


def square_kernel(*refs):
    *refs, out = refs
    out[:, 0:1] = square_sum(refs[0], refs[1])
    total = square_sum(refs[2], refs[3])
    for index in range(4, len(refs), 2):
        total += square_sum(refs[index], refs[index + 1])
    out[:, 1:2] = total


def mixed_kernel(slots, first, sections, here, proc, sizes, x_keep, keep_attn, got_attn, *rest):
    ssm_refs = rest[: 2 * sections]
    own_squares, other_squares, gains, features = rest[2 * sections : 2 * sections + 4]
    outs = rest[2 * sections + 4 : 2 * sections + 4 + here]
    made, sems = rest[2 * sections + 4 + here :]
    step = pl.program_id(0)
    ssm = jnp.concatenate(
        [
            keep[...].astype(jnp.float32) + got[...].astype(jnp.float32)
            for keep, got in zip(ssm_refs[::2], ssm_refs[1::2])
        ],
        axis=1,
    )
    attn = keep_attn[...].astype(jnp.float32) + got_attn[...].astype(jnp.float32)
    scales = lax.rsqrt((own_squares[...] + other_squares[...]) / D + EPSILON)
    branch = 0.5 * (
        gains[0:1, :] * attn * scales[:, 0:1] + gains[1:2, :] * ssm * scales[:, 1:2]
    )
    mixed = (x_keep[...].astype(jnp.float32) + branch).astype(jnp.bfloat16)
    placed = exact_dot(mixed, features[...])
    size = made.shape[1]
    in_step = mixed.shape[0] // size
    outward = row_mover(slots, size // slots, False)
    slot = lax.broadcasted_iota(jnp.int32, (size, 1), 0) // (size // slots)

    def copy(number):
        return pltpu.make_async_copy(made.at[number], outs[number], sems.at[number])

    for index in range(in_step):
        number = step * in_step + index
        rows = exact_dot(outward, placed[index * size : (index + 1) * size])
        live = slot < sizes[proc[first + number]]
        made[number] = jnp.where(live, rows, jnp.zeros_like(rows))
    for number in range(here):

        @pl.when(step == number // in_step)
        def _(number=number):
            copy(number).start()

    @pl.when(step == here // in_step - 1)
    def _():
        for number in range(here):
            copy(number).wait()


def local(
    tokens,
    prefix_kv,
    ssm_state,
    conv_state,
    prefix_len,
    group_size,
    serve_replica,
    in_gain,
    w_query,
    w_keyval,
    w_inner,
    conv_weight,
    conv_bias,
    w_xproj,
    dt_weight,
    dt_bias,
    decay_log,
    skip_gain,
    w_attn_out,
    w_ssm_out,
    attn_gain,
    ssm_gain,
):
    rep_count = lax.axis_size("rep")
    row_axis = lax.axis_size("tr")
    tensor_count = lax.axis_size("tc")
    rep = lax.axis_index("rep")
    row = lax.axis_index("tr")
    core = lax.axis_index("tc")
    groups, slots, steps, width = tokens.shape
    pairs = groups // rep_count
    kv_here = KVH // tensor_count
    per_kv = QH // KVH
    heads_width = QH // tensor_count * HD
    group_rows = slots * steps
    rows = groups * group_rows
    tile = groups // 4 * group_rows
    channels = w_inner.shape[2]
    shards = rep_count * row_axis
    shard = w_query.shape[0]
    pad = -(-shard // 8) * 8
    depth = shards * pad
    half = depth // 2
    wide = -(-half // 128) * 128
    by_links = rep_count == 4 and row_axis == 4
    sections = 2 if by_links else 1
    section = half // sections
    section_wide = -(-section // 128) * 128
    columns = sections * section_wide
    bf16 = jnp.bfloat16
    f32 = jnp.float32
    i32 = jnp.int32

    def padded(value):
        return jnp.pad(value, ((0, pad - shard), (0, 0)))

    ssm_shard = padded(w_ssm_out.T)
    conv_shard = padded(w_inner[:, 0])
    def shard_behind(w_query, w_keyval, w_attn_out, w_gate):
        return padded(jnp.concatenate([w_query, w_keyval, w_attn_out.T, w_gate], axis=1))

    qkv_width = w_query.shape[1] + w_keyval.shape[1]
    attn_width = qkv_width + heads_width
    rank, states = dt_weight.shape[0], decay_log.shape[0]
    mixes = 256

    def feature_at(column, lines_outside, rep, row):
        inside = column < half
        if lines_outside:
            inside = column % section_wide < section
            column = column // section_wide * section + column % section_wide
        block, offset = column // pad, column % pad
        if by_links:
            if lines_outside:
                slot, plane = block // 2, block % 2
            else:
                slot, plane = block % row_axis, block // row_axis
            low = row < 2
            line = jnp.where(
                slot == 0,
                row,
                jnp.where(
                    slot == 1,
                    row ^ 1,
                    jnp.where(slot == 2, jnp.where(low, 2, 1), jnp.where(low, 3, 0)),
                ),
            )
            block = ((rep % 2) ^ plane) * row_axis + line
        return jnp.where((offset < shard) & inside, block * shard + offset, -1)

    def picker(shape, column_dim, lines_outside, rep, row):
        line = tuple(size if dim == column_dim else 1 for dim, size in enumerate(shape))
        column = lax.broadcasted_iota(i32, line, column_dim)
        (source,) = tie(feature_at(column, lines_outside, rep, row))
        return lax.broadcasted_iota(i32, shape, 1 - column_dim) == source

    def column_picks(rep, row):
        keep_pick = picker((width, columns), 1, True, rep, row)
        gains = jnp.stack([attn_gain, ssm_gain])
        gains = lax.dynamic_slice_in_dim(gains, core * width, width, 1)
        gains = jnp.sum(jnp.where(keep_pick[None], gains[:, :, None], 0.0), axis=1)
        features_back = picker((columns, width), 0, True, rep, row).astype(bf16)
        return keep_pick.astype(bf16), gains, features_back

    second = ((rep // 2) ^ core if by_links else core).astype(i32)[None]

    def group_order(serve_replica):
        served = lax.dynamic_slice_in_dim(serve_replica, first_group, groups, 0)
        target = served ^ rep if by_links else served
        ids = jnp.arange(groups, dtype=i32)
        same = (served[:, None] == served[None, :]) & (ids[None, :] < ids[:, None])
        places = jnp.sum(same.astype(i32), axis=1) * rep_count + target
        return jnp.sum(
            jnp.where(places[None, :] == ids[:, None], ids[None, :], 0), axis=1
        ).astype(i32)

    def inverse_rms(tokens):
        wide_rows = tokens.reshape(groups, group_rows, width).astype(f32)
        square_sums = lax.psum(jnp.sum(wide_rows * wide_rows, axis=2), "tc")
        return lax.rsqrt(square_sums / D + EPSILON)[:, :, None]

    first_group = (rep * row_axis + row) * groups
    def row_block(columns, size=tile, first=0):
        return pl.BlockSpec((size, columns), lambda g, *_: (g + first, 0))

    def whole(*shape):
        return pl.BlockSpec(shape, lambda g, *_: (0,) * len(shape))

    def group_block(*shape, first=0):
        return pl.BlockSpec(
            (1,) + shape, lambda g, proc, *_: (proc[g + first],) + (0,) * len(shape)
        )

    anywhere = pl.BlockSpec(memory_space=pl.ANY)

    def rows_of(columns, kind=bf16, count=rows):
        return jax.ShapeDtypeStruct((count, columns), kind)

    def call(kernel, scalars, grid, in_specs, out_specs, out_shape, scratch, spend, name, alias=None):
        return pl.pallas_call(
            kernel,
            grid_spec=pltpu.PrefetchScalarGridSpec(
                num_scalar_prefetch=scalars,
                grid=(grid,),
                in_specs=in_specs,
                out_specs=out_specs,
                scratch_shapes=scratch,
            ),
            out_shape=out_shape,
            input_output_aliases=alias or {},
            compiler_params=params(),
            cost_estimate=cost(spend * 1.0e7, rows * 4),
            name=name,
        )

    def piece_copies(pieces):
        return pltpu.SemaphoreType.DMA((max(len(pieces), 2),))

    def spread(inv, rep, row):
        spread_pick = picker((width, wide), 1, False, rep, row).astype(bf16)
        return call(
            functools.partial(spread_kernel, slots),
            1,
            groups,
            [
                group_block(group_rows, width),
                group_block(group_rows, 1),
                whole(1, width),
                whole(width, wide),
            ],
            row_block(wide, group_rows),
            rows_of(wide),
            [],
            8,
            "spread_rows",
        )(proc, tokens.reshape(groups, group_rows, width), inv, in_gain[None], spread_pick)

    def place(keep_pick):
        return call(
            functools.partial(place_kernel, slots),
            1,
            groups,
            [group_block(group_rows, width), whole(width, columns)],
            row_block(columns, group_rows),
            rows_of(columns),
            [],
            8,
            "place_rows",
        )(proc, tokens.reshape(groups, group_rows, width), keep_pick)

    def attention(rows_own, rows_other, pieces, lengths):
        return call(
            functools.partial(
                attention_kernel, slots, group_rows, kv_here, per_kv, len(pieces), half, 0
            ),
            3,
            rows // tile,
            [row_block(wide)] * 2 + [whole(*prefix_kv.shape)] + [anywhere] * len(pieces),
            row_block(heads_width),
            rows_of(heads_width),
            [pltpu.VMEM((2 * wide, qkv_width), bf16), piece_copies(pieces)],
            15,
            "attention",
        )(proc, lengths, second, rows_own, rows_other, prefix_kv, *pieces)

    def small_operands(w_xproj, conv_state, conv_bias, dt_bias, skip_gain, prefix_len, group_size):
        mix_weight = jnp.concatenate(
            [
                jnp.pad(w_xproj[:, :rank], ((0, 0), (0, 128 - rank))),
                jnp.pad(w_xproj[:, rank:], ((0, 0), (0, mixes - 128 - 2 * states))),
            ],
            axis=1,
        )
        return (
            mix_weight,
            conv_state,
            conv_bias[None],
            dt_bias[None],
            skip_gain[None],
            lax.dynamic_slice_in_dim(prefix_len, first_group, groups, 0),
            lax.dynamic_slice_in_dim(group_size, first_group, groups, 0),
        )

    plain = (w_xproj, conv_state, conv_bias, dt_bias, skip_gain, prefix_len, group_size)

    def convolve(rows_own, rows_other, pieces, small):
        return call(
            functools.partial(conv_kernel, slots, group_rows, len(pieces), half, 0),
            2,
            rows // tile,
            [
                row_block(wide),
                row_block(wide),
                whole(*conv_state.shape),
                whole(*conv_weight.shape),
                whole(1, channels),
                whole(channels, mixes),
            ]
            + [anywhere] * len(pieces),
            [row_block(channels), row_block(mixes)],
            [rows_of(channels), rows_of(mixes)],
            [pltpu.VMEM((2 * wide, channels), bf16), piece_copies(pieces)],
            14,
            "convolve",
        )(
            proc,
            second,
            rows_own,
            rows_other,
            small[1],
            conv_weight,
            small[2],
            small[0],
            *pieces,
        )

    def scan(first, count, conv_out, mix_own, mix_other, small, earlier=()):
        across = -(-channels // 128) * 128
        blocks = functools.partial(row_block, size=group_rows, first=first)
        return call(
            functools.partial(scan_kernel, slots),
            1,
            count,
            [
                blocks(channels),
                blocks(mixes),
                blocks(mixes),
                whole(rank, channels),
                whole(1, channels),
                whole(states, channels),
                whole(1, channels),
                group_block(*ssm_state.shape[1:], first=first),
            ]
            + [anywhere] * len(earlier),
            blocks(channels),
            rows_of(channels, f32),
            [pltpu.VMEM((group_rows, across), f32)] * 3
            + [pltpu.VMEM((states, across), f32)] * 2
            + [pltpu.VMEM((states, group_rows, 128), bf16)] * 2,
            4 * count,
            "scan_states",
            {9: 0} if earlier else None,
        )(
            proc,
            conv_out,
            mix_own,
            mix_other,
            dt_weight,
            small[3],
            decay_log,
            small[4],
            ssm_state,
            *earlier,
        )

    def gate(rows_own, rows_other, scanned, pieces, first_column):
        return call(
            functools.partial(gate_kernel, len(pieces), half, first_column),
            1,
            rows // tile,
            [row_block(wide)] * 2 + [row_block(channels)] + [anywhere] * len(pieces),
            row_block(channels),
            rows_of(channels),
            [pltpu.VMEM((2 * wide, channels), bf16), piece_copies(pieces)],
            13,
            "gate",
        )(second, rows_own, rows_other, scanned, *pieces)

    def attn_out(heads, pieces):
        blocks = []
        for number in range(sections):
            if by_links:
                blocks += [
                    ((plane * row_axis + slot) * pad, pad)
                    for slot in (2 * number, 2 * number + 1)
                    for plane in range(2)
                ]
            else:
                blocks.append((0, half))
            if section_wide > section:
                blocks.append((None, section_wide - section))
        return call(
            functools.partial(attn_out_kernel, len(pieces), half, qkv_width, tuple(blocks)),
            1,
            rows // tile,
            [row_block(heads_width)] + [anywhere] * len(pieces),
            [row_block(columns)] * 2,
            [rows_of(columns)] * 2,
            [
                pltpu.VMEM((2 * wide, heads_width), bf16),
                pltpu.VMEM((2 * columns, heads_width), bf16),
                piece_copies(pieces),
            ],
            6,
            "attn_out",
        )(second, heads, *pieces)

    def ssm_out(gated, choices, pieces):
        scalars = jnp.stack([second[0], inner.astype(i32) if by_links else second[0]])
        return call(
            functools.partial(ssm_out_kernel, choices, section // len(choices)),
            1,
            rows // tile,
            [row_block(channels)] + [anywhere] * len(pieces),
            [row_block(section_wide)] * 2,
            [rows_of(section_wide)] * 2,
            [
                pltpu.VMEM((2 * section_wide, channels), bf16),
                pltpu.SemaphoreType.DMA((len(choices), 2)),
            ],
            8,
            "ssm_out",
        )(scalars, gated, *pieces)

    def squares(attn, ssm):
        return call(
            square_kernel,
            0,
            rows // tile,
            [row_block(columns)] * 2 + [row_block(section_wide)] * len(ssm),
            row_block(2),
            rows_of(2, f32),
            [],
            2,
            "squares",
        )(*attn, *ssm)

    def mix(part, x_keep, attn, ssm, own_squares, other_squares, gains, features_back, sizes):
        here = groups // pairs
        size = 2 * group_rows
        block = functools.partial(row_block, size=size, first=part * here // 2)
        return call(
            functools.partial(mixed_kernel, slots, part * here, sections, here),
            2,
            here // 2,
            [block(columns)] * 3
            + [block(section_wide)] * (2 * sections)
            + [block(2)] * 2
            + [whole(2, columns), whole(columns, width)],
            [anywhere] * here,
            [rows_of(width, count=group_rows)] * here,
            [pltpu.VMEM((here, group_rows, width), bf16), pltpu.SemaphoreType.DMA((here,))],
            4,
            "mixed_rows",
        )(
            proc,
            sizes,
            x_keep,
            *attn,
            *ssm,
            own_squares,
            other_squares,
            gains,
            features_back,
        )

    if by_links:

        def line_first(value):
            return along_z(value, Z_OUTER), along_z(value, Z_INNER)

        def line_second(first):
            near, middle = first
            return along_z(near, Z_INNER), along_z(middle, Z_ENDS), along_z(near, Z_FAR)

        inner = (row == 1) | (row == 2)

        def line_block(value, first, last):
            near, middle = first
            crossed, ends, far = last
            return jnp.concatenate(
                [value, near, jnp.where(inner, middle, ends), jnp.where(inner, crossed, far)],
                axis=0,
            )

        def plane_first(value):
            return swap_x(value), swap_y(value)

        def plane_second(first):
            by_x, by_y = first
            cut = by_x.shape[0] // 16 * 8
            return swap_y(by_x[:cut]), swap_x(by_y[cut:])

        def upper(value, first):
            return jnp.concatenate([value, first[0]], axis=0)

        def lower(first, last):
            crossed, ends, far = last
            return jnp.concatenate(
                [jnp.where(inner, first[1], ends), jnp.where(inner, crossed, far)], axis=0
            )

        def left(values):
            return tuple(value[:, :attn_width] for value in values)

        def right(values):
            return tuple(value[:, attn_width:] for value in values)

        ssm_corner = lax.ppermute(ssm_shard, "rep", D_PAIRS)
        ssm_late, conv_shard = tie(ssm_shard, conv_shard)
        ssm_plane = plane_first(ssm_late) + (ssm_corner,)
        conv_z1 = line_first(conv_shard)
        inv_rms = inverse_rms(tokens)

        (
            conv_z1,
            conv_shard,
            ssm_plane,
            inv_rms,
            serve_late,
            rep_late,
            row_late,
            late_weights,
        ) = tie(
            conv_z1,
            conv_shard,
            ssm_plane,
            inv_rms,
            serve_replica,
            rep,
            row,
            (w_query, w_keyval, w_attn_out, w_inner[:, 1]),
        )
        conv_z2 = line_second(conv_z1)
        conv_top_own = upper(conv_shard, conv_z1)
        conv_top = plane_first(conv_top_own)
        proc = group_order(serve_late)
        rows_own = spread(inv_rms, rep_late, row_late)
        back_shard = shard_behind(*late_weights)

        conv_bottom_own = lower(conv_z1, conv_z2)
        conv_top, conv_bottom_own, back_shard, rows_own, plain, rep_late, row_late = tie(
            conv_top, conv_bottom_own, back_shard, rows_own, plain, rep, row
        )
        conv_bottom = plane_first(conv_bottom_own)
        back_z1 = line_first(back_shard)
        rows_other = other_core(rows_own)
        small = small_operands(*plain)
        picks = column_picks(rep_late, row_late)

        conv_top, conv_bottom, back_z1, small, rows_other, ssm_plane, picks = tie(
            conv_top, conv_bottom, back_z1, small, rows_other, ssm_plane, picks
        )
        keep_pick, gains, features_back = picks
        conv_corner = (swap_y(conv_top[0]), swap_x(conv_bottom[1]))
        back_z2 = line_second(back_z1)
        ssm_block = jnp.concatenate((ssm_shard,) + ssm_plane, axis=0)
        x_keep = place(keep_pick)

        conv_corner, ssm_block, x_keep, gains, features_back = tie(
            conv_corner, ssm_block, x_keep, gains, features_back
        )
        conv_out, mix_own = convolve(
            rows_own,
            rows_other,
            (conv_top_own, conv_bottom_own, conv_top[0], conv_bottom[0], conv_top[1], conv_bottom[1])
            + conv_corner,
            small,
        )

        conv_out, mix_own, back_z2, ssm_block = tie(conv_out, mix_own, back_z2, ssm_block)
        gate_block = line_block(right((back_shard,))[0], right(back_z1), right(back_z2))
        gate_p1 = plane_first(gate_block)
        ssm_near, ssm_middle = line_first(ssm_block)
        mix_other = other_core(mix_own)
        count = groups // 2
        scanned = scan(0, count, conv_out, mix_own, mix_other, small)

        gate_p1, scanned = tie(gate_p1, scanned)
        gate_p2 = plane_second(gate_p1)
        quarter = groups // 4
        scanned = scan(count, quarter, conv_out, mix_own, mix_other, small, (scanned,))
        scanned, ssm_near, ssm_middle = tie(scanned, ssm_near, ssm_middle)
        crossed = along_z(ssm_near, Z_INNER)
        ends = along_z(ssm_middle, Z_ENDS)
        scanned = scan(
            count + quarter, quarter, conv_out, mix_own, mix_other, small, (scanned,)
        )
        attn_block = line_block(left((back_shard,))[0], left(back_z1), left(back_z2))

        gate_p2, attn_block, scanned = tie(gate_p2, attn_block, scanned)
        attn_p1 = plane_first(attn_block)
        gated = gate(
            rows_own, rows_other, scanned, (gate_block,) + tuple(gate_p1) + tuple(gate_p2), 0
        )

        attn_p1, gated = tie(attn_p1, gated)
        attn_p2 = plane_second(attn_p1)
        keep_early, send_early = ssm_out(gated, (1, 1), (ssm_block, ssm_near))
        attn_p2, keep_early, crossed, ends, ssm_near = tie(
            attn_p2, keep_early, crossed, ends, ssm_near
        )
        far = along_z(ssm_near, Z_FAR)
        got_early = other_core(send_early)
        attn_pieces = (attn_block,) + tuple(attn_p1) + tuple(attn_p2)
        heads = attention(rows_own, rows_other, attn_pieces, small[5])
        keep_attn, send_attn = attn_out(heads, attn_pieces)
        send_attn, far = tie(send_attn, far)
        got_attn = other_core(send_attn)
        attn = [keep_attn, got_attn]

        late_pieces = (ssm_middle, ends, crossed, far)
        keep_late, send_late = ssm_out(gated, (2, 2), late_pieces)
        got_late = other_core(send_late)
        ssm = [keep_early, got_early, keep_late, got_late]
        sums = squares(attn, ssm)
        other_sums = other_core(sums)
        received = []
        for part in range(pairs):
            mixed = mix(part, x_keep, attn, ssm, sums, other_sums, gains, features_back, small[6])
            received.append(
                (
                    mixed[0],
                    swap_x(mixed[1]),
                    swap_y(mixed[2]),
                    lax.ppermute(mixed[3], "rep", D_PAIRS),
                )
            )
        by_source = [jnp.stack([part[index] for part in received]) for index in range(rep_count)]
        for bit in (1, 2):
            swapped = (rep & bit) != 0
            by_source = [
                jnp.where(swapped, by_source[index ^ bit], by_source[index])
                for index in range(rep_count)
            ]
        mixed = jnp.concatenate(by_source, axis=0)
    else:

        def gathered(value):
            return lax.all_gather(value, ("rep", "tr"), axis=0, tiled=True)

        proc = group_order(serve_replica)
        small = small_operands(*plain)
        rows_own = spread(inverse_rms(tokens), rep, row)
        rows_other = other_core(rows_own)
        keep_pick, gains, features_back = column_picks(rep, row)
        x_keep = place(keep_pick)
        attn_pieces = (gathered(shard_behind(w_query, w_keyval, w_attn_out, w_inner[:, 1])),)
        heads = attention(rows_own, rows_other, attn_pieces, small[5])
        conv_out, mix_own = convolve(rows_own, rows_other, (gathered(conv_shard),), small)
        scanned = scan(0, groups, conv_out, mix_own, other_core(mix_own), small)
        gated = gate(rows_own, rows_other, scanned, attn_pieces, attn_width)
        keep_attn, send_attn = attn_out(heads, attn_pieces)
        attn = [keep_attn, other_core(send_attn)]
        kept, sent = ssm_out(gated, (1,), (gathered(ssm_shard),))
        ssm = [kept, other_core(sent)]
        sums = squares(attn, ssm)
        other_sums = other_core(sums)
        received = [
            jnp.stack(
                mix(part, x_keep, attn, ssm, sums, other_sums, gains, features_back, small[6])
            )
            for part in range(pairs)
        ]
        mixed = jnp.stack(received, axis=1).reshape(groups, group_rows, width)
        mixed = lax.all_to_all(mixed, "rep", split_axis=0, concat_axis=0, tiled=True)
    return mixed.reshape(groups, slots, steps, width)


def solution(mesh):
    placed = (
        P(("rep", "tr"), None, None, "tc"),
        P(("rep", "tr"), None, "tc"),
        P(("rep", "tr"), None, "tc"),
        P(("rep", "tr"), None, "tc"),
        P(),
        P(),
        P(),
        P("tc"),
        P(("rep", "tr"), "tc"),
        P(("rep", "tr"), "tc"),
        P(("rep", "tr"), None, "tc"),
        P(None, "tc"),
        P("tc"),
        P("tc", None),
        P(None, "tc"),
        P("tc"),
        P(None, "tc"),
        P("tc"),
        P("tc", ("rep", "tr")),
        P("tc", ("rep", "tr")),
        P(),
        P(),
    )
    return jax.shard_map(
        local,
        mesh=mesh,
        in_specs=placed,
        out_specs=P(("rep", "tr"), None, None, "tc"),
        check_vma=False,
    )
```
